32 devices in a mesh: expert: 8 (over y, x, core), shard: 4 (over z).
Axes of the slice: x: 2, y: 2, z: 4, core: 2. Of those that a mesh axis runs over, the one named last changes fastest.
Arguments:
- block_in: bfloat16 [4096, 2048], P(('expert', 'shard')), may hold values from -6 to 6
- cotangent: bfloat16 [4096, 2048], P(('expert', 'shard')), may hold values from -6 to 6
- doc_ids: int32 [8, 512], P('expert'), may hold values from 0 to 2, never falling along the last dimension, each value on 1 to 384 neighbouring positions
- routes: int32 [4096, 6], P(('expert', 'shard')), may hold values from 0 to 15, all different within a row; in each aligned block of 128 rows (0 to 127, 128 to 255, ...) at most 64 rows name the same one
- attn_gain: bfloat16 [2048], P('shard'), may hold values from 0.25 to 1.75
- query_weight: bfloat16 [2048, 3072], P('shard'), may hold values from -1 to 1
- kv_down_weight: bfloat16 [2048, 576], P('shard'), may hold values from -0.125 to 0.125
- kv_gain: bfloat16 [512], P('shard'), may hold values from 0.25 to 1.75
- kv_up_weight: bfloat16 [512, 4096], P('shard'), may hold values from -0.25 to 0.25
- out_weight: bfloat16 [2048, 2048], P('shard'), may hold values from -1 to 1
- ffn_gain: bfloat16 [2048], P('shard'), may hold values from 0.25 to 1.75
- router_weight: bfloat16 [2048, 16], P('shard'), may hold values from -1 to 1
- shared_in: bfloat16 [2048, 5632], P('shard'), may hold values from -0.125 to 0.125
- shared_down: bfloat16 [2816, 2048], P('shard'), may hold values from -0.21875 to 0.21875
- expert_in: bfloat16 [16, 4096, 1408], P('expert', None, 'shard'), may hold values from -0.125 to 0.125
- expert_down: bfloat16 [16, 2048, 1408], P('expert', None, 'shard'), may hold values from -0.3125 to 0.3125
Outputs:
- block_out: float32 [4096, 2048], P(('expert', 'shard'))
- input_grad: float32 [4096, 2048], P(('expert', 'shard'))
- attn_gain_grad: float32 [2048], P(('expert', 'shard'))
- query_weight_grad: float32 [2048, 3072], P(('expert', 'shard'))
- kv_down_weight_grad: float32 [2048, 576], P(('expert', 'shard'))
- kv_gain_grad: float32 [512], P(('expert', 'shard'))
- kv_up_weight_grad: float32 [512, 4096], P(('expert', 'shard'))
- out_weight_grad: float32 [2048, 2048], P(('expert', 'shard'))
- ffn_gain_grad: float32 [2048], P(('expert', 'shard'))
- router_weight_grad: float32 [2048, 16], P(('expert', 'shard'))
- shared_in_grad: float32 [2048, 5632], P(('expert', 'shard'))
- shared_down_grad: float32 [2816, 2048], P(('expert', 'shard'))
- expert_in_grad: float32 [16, 4096, 1408], P('expert', None, 'shard')
- expert_down_grad: float32 [16, 2048, 1408], P('expert', None, 'shard')
The draws below stay inside these ranges and needn't reach their ends.
Inputs may be any that keep to these rules, and one draw needn't show every extreme that they name: `routes`: within the rows of one device (128 tokens) every expert is named at most 64 times. `doc_ids`: in each group the document numbers never fall and run through 0 to 2; a document has 1 to 384 tokens and one has exactly 384.
All inputs are finite; a program needn't handle non-finite values.
Results may differ from the reference program's by a relative error of at most 0.02.
Values may be sent and summed in bfloat16 or wider, within the bound.
A program may use at most 512 MiB of HBM per device.

```python
import math
import jax
import jax.numpy as jnp
import numpy as np
from jax import lax

D = 2048
HEADS = 16
NOPE = 128
ROPE = 64
VDIM = 128
KV_RANK = 512
FF_E = 1408
SH_FF = 2816
TOP = 6
TOK_DEV = 128
DOCS = 3
EXPERTS = 16
TOKENS = 4096
GROUPS = 8
GROUP_TOK = 512
SEQ_MOST = 384
CAP = 64


def draw_query_weight(key, part):
    base_key = jax.random.fold_in(key, 11)
    columns = HEADS * (NOPE + ROPE)
    base_draw = jax.random.truncated_normal(base_key, -4.0, 4.0, (D, columns), jnp.float32)
    return (base_draw * D ** (-0.5)).astype(jnp.bfloat16)


def draw_router_weight(key, part):
    base_key = jax.random.fold_in(key, 23)
    base_draw = jax.random.truncated_normal(base_key, -4.0, 4.0, (D, EXPERTS), jnp.float32) * 0.5
    return (base_draw * D ** (-0.5)).astype(jnp.bfloat16)


def level_of(stream_key, shape, shards, smallest, largest):
    def one(axis_at, shards_of):
        steps = jax.random.uniform(jax.random.fold_in(jax.random.fold_in(stream_key, 6), axis_at), (shards_of,), jnp.float32, smallest / len(shards), largest / len(shards))
        return jnp.repeat(jnp.exp(steps), shape[axis_at] // shards_of).reshape((-1,) + (1,) * (len(shape) - axis_at - 1))

    factor_of = one(*shards[0])
    for cut in shards[1:]:
        factor_of = factor_of * one(*cut)
    return factor_of


def profile(number_of, total, most, skew):
    weights = [(1 << 20) // math.isqrt(standing ** skew) + 1 for standing in range(2, number_of + 1)]
    rest, given = total - most - (number_of - 1), [1] * (number_of - 1)
    while rest > 0:
        candidates = [i for i in range(number_of - 1) if given[i] < most]
        pool, remaining = sum([weights[i] for i in candidates]), rest
        for i in candidates:
            more = min(most - given[i], max(1, remaining * weights[i] // pool), rest)
            given[i] = given[i] + more
            rest = rest - more
    return np.array([most] + given)


def uneven(stream_key, count, total, most, lean):
    if count == 2:
        one = jax.random.randint(stream_key, (), max(1, total - most), min(most, total - 1) + 1)
        return jnp.stack([one, total - one])
    tallies = jnp.asarray(profile(count, total, most, lean), jnp.int32)
    twos = (count - 1) // 2
    donor, taker = tallies[1:1 + 2 * twos:2], tallies[2:2 + 2 * twos:2]
    room = jnp.minimum(donor - 1, most - taker)
    moved = jax.random.randint(jax.random.fold_in(stream_key, 1), (twos,), 0, 1 << 20) % (room + 1)
    tallies = tallies.at[1:1 + 2 * twos:2].set(donor - moved).at[2:2 + 2 * twos:2].set(taker + moved)
    return tallies[jax.random.permutation(jax.random.fold_in(stream_key, 2), count)]


def routed_block(stream_key, own, number, rows, number_of, top, limit, lean):
    sequence = jax.random.permutation(stream_key, number_of)
    heavy_load, usual = portions_of(number_of, rows * top, limit, lean, True), portions_of(number_of, rows * top, limit, lean, False)
    places = jnp.arange(number_of)

    def named(sizes, turn):
        used = int((sizes > 0).sum())
        fixed = max(1, used // 4)
        passed = fixed + (places - fixed + turn * (used - fixed)) % max(1, number_of - fixed)
        return jnp.zeros((number_of,), jnp.int32).at[sequence[jnp.where(places < fixed, places, passed)]].set(jnp.asarray(sizes, jnp.int32))

    sizes = jnp.where(number % 4 == 0, named(heavy_load, number // 4), named(usual, number - number // 4 - 1))
    mixed = jax.random.permutation(jax.random.fold_in(own, 3), number_of)
    giver, sink = mixed[0:number_of // 2 * 2:2], mixed[1:number_of // 2 * 2:2]
    margin = jnp.minimum(sizes[giver] - 1, limit - sizes[sink]) // 2
    margin = jnp.where((giver == sequence[0]) | (sink == sequence[0]) | (sizes[sink] == 0), 0, jnp.maximum(margin, 0))
    passed = jax.random.randint(jax.random.fold_in(own, 4), (number_of // 2,), 0, 1 << 20) % (margin + 1)
    sizes = sizes.at[giver].add(-passed).at[sink].add(passed)
    items = jnp.searchsorted(jnp.cumsum(sizes), jnp.arange(rows * top), side="right").astype(jnp.int32)
    table = items.reshape(top, rows).T
    table = table[jax.random.permutation(jax.random.fold_in(own, 1), rows)]
    turn = jax.random.randint(jax.random.fold_in(own, 2), (rows, 1), 0, top)
    return jnp.take_along_axis(table, (jnp.arange(top)[None, :] + turn) % top, axis=1)


def portions_of(count, total, reach, lean, full):
    loads = [(1 << 20) // math.isqrt(grade ** lean) + 1 for grade in range(1, count + 1)]
    largest = reach if full else min(reach, max(-(-total // count), total * loads[0] // sum(loads)))
    least = 1 if total - largest >= count - 1 else 0
    counts, surplus = [largest] + [least] * (count - 1), total - largest - least * (count - 1)
    while surplus > 0:
        candidates = [i for i in range(1, count) if counts[i] < largest] or [i for i in range(1, count) if counts[i] < reach]
        mass, left = sum([loads[i] for i in candidates]), surplus
        for i in candidates:
            extra = min(reach - counts[i], max(1, left * loads[i] // mass), surplus)
            counts[i] = counts[i] + extra
            surplus = surplus - extra
    return np.array(counts)


def gaussian(key, dims, width, most, shards=(), kind=jnp.bfloat16):
    factor_of = level_of(key, dims, shards, -0.22, 0.18) if shards else 1.0
    drawn = jax.random.normal(key, dims, jnp.float32) * width * factor_of
    return jnp.minimum(jnp.maximum(drawn, -most), most).astype(kind)


def setup_inputs(seed: int = 0) -> dict:
    streams_of = jax.random.split(jax.random.key(seed), 17)
    block_in = gaussian(streams_of[0], (TOKENS, D), 1.0, 6.0, ((0, 32),))
    cotangent = gaussian(streams_of[1], (TOKENS, D), 1.0, 6.0, ((0, 32),))
    doc_ids = jax.vmap(lambda own: jnp.searchsorted(jnp.cumsum(uneven(own, DOCS, GROUP_TOK, SEQ_MOST, 1)), jnp.arange(GROUP_TOK), side="right"))(jax.random.split(streams_of[2], GROUPS)).reshape((GROUPS, GROUP_TOK)).astype(jnp.int32)
    routes_keys = jax.random.split(jax.random.fold_in(streams_of[3], 1), TOKENS // TOK_DEV)
    routes_turns = jax.random.permutation(jax.random.fold_in(streams_of[3], 3), TOKENS // TOK_DEV)
    routes = jax.vmap(lambda own, number: routed_block(jax.random.fold_in(streams_of[3], 2), own, number, TOK_DEV, EXPERTS, TOP, CAP, 2))(routes_keys, routes_turns).reshape((TOKENS, TOP))
    attn_gain = jnp.clip(1.0 + 0.15 * jax.random.normal(streams_of[4], (D,), jnp.float32), 0.25, 1.75).astype(jnp.bfloat16)
    query_weight = draw_query_weight(jax.random.fold_in(streams_of[16], 71), 0)
    kv_down_weight = gaussian(streams_of[6], (D, KV_RANK + ROPE), D ** -0.5, 0.125, ((0, 4),))
    kv_gain = jnp.clip(1.0 + 0.15 * jax.random.normal(streams_of[7], (KV_RANK,), jnp.float32), 0.25, 1.75).astype(jnp.bfloat16)
    kv_up_weight = gaussian(streams_of[8], (KV_RANK, HEADS * (NOPE + VDIM)), KV_RANK ** -0.5, 0.25, ((0, 4),))
    out_weight = gaussian(streams_of[9], (HEADS * VDIM, D), (HEADS * VDIM // 64) ** -0.5, 1.0, ((0, 4),))
    ffn_gain = jnp.clip(1.0 + 0.15 * jax.random.normal(streams_of[10], (D,), jnp.float32), 0.25, 1.75).astype(jnp.bfloat16)
    router_weight = draw_router_weight(jax.random.fold_in(streams_of[16], 71), 0)
    shared_in = gaussian(streams_of[12], (D, 2 * SH_FF), D ** -0.5, 0.125, ((0, 4),))
    shared_down = gaussian(streams_of[13], (SH_FF, D), (SH_FF // 4) ** -0.5, 0.21875, ((0, 4),))
    expert_in = gaussian(streams_of[14], (EXPERTS, 2 * D, FF_E), D ** -0.5, 0.125, ((0, 8), (2, 4)))
    expert_down = gaussian(streams_of[15], (EXPERTS, D, FF_E), (FF_E // 4) ** -0.5, 0.3125, ((0, 8), (2, 4)))
    return dict(block_in=block_in, cotangent=cotangent, doc_ids=doc_ids, routes=routes, attn_gain=attn_gain, query_weight=query_weight, kv_down_weight=kv_down_weight, kv_gain=kv_gain, kv_up_weight=kv_up_weight, out_weight=out_weight, ffn_gain=ffn_gain, router_weight=router_weight, shared_in=shared_in, shared_down=shared_down, expert_in=expert_in, expert_down=expert_down)


EPS = 1e-06
ROPE_BASE = 10000.0
HIGHEST = lax.Precision.HIGHEST

def inv_rms(values):
    return lax.rsqrt(lax.optimization_barrier(jnp.mean(values * values, axis=-1, keepdims=True)) + EPS)

def norm_back(grad_out, values, inv_scale, gain_row):
    scaled = grad_out * gain_row
    grad_in = inv_scale * scaled - values * inv_scale ** 3 * lax.optimization_barrier(jnp.mean(scaled * values, axis=-1, keepdims=True))
    grad_gain = lax.optimization_barrier(jnp.sum(grad_out * values * inv_scale, axis=0))
    return (grad_in, grad_gain)

def silu_parts(pre_act):
    sigmoid_val = jax.nn.sigmoid(pre_act)
    return (pre_act * sigmoid_val, sigmoid_val * (1.0 + pre_act * (1.0 - sigmoid_val)))

def doc_positions(doc_row):
    index_row = jnp.arange(doc_row.shape[0], dtype=jnp.int32)
    starts = jnp.concatenate([jnp.ones((1,), dtype=bool), doc_row[1:] != doc_row[:-1]])
    begin_at = lax.cummax(jnp.where(starts, index_row, 0), axis=0)
    return index_row - begin_at

def rope_tables(positions):
    half_width = ROPE // 2
    frequency = ROPE_BASE ** (-jnp.arange(half_width, dtype=jnp.float32) / half_width)
    angles = positions.astype(jnp.float32)[:, None] * frequency[None, :]
    return (jnp.cos(angles), jnp.sin(angles))

def rotate(values, cosine, sine_table):
    half_width = cosine.shape[-1]
    front_half = values[..., :half_width]
    back_half = values[..., half_width:]
    return jnp.concatenate([front_half * cosine - back_half * sine_table, back_half * cosine + front_half * sine_table], axis=-1)

def unrotate(values, cosine, sine_table):
    half_width = cosine.shape[-1]
    front_half = values[..., :half_width]
    back_half = values[..., half_width:]
    return jnp.concatenate([front_half * cosine + back_half * sine_table, back_half * cosine - front_half * sine_table], axis=-1)

def product(pattern, left, right):
    return jnp.einsum(pattern, left.astype(jnp.float32), right.astype(jnp.float32), precision=HIGHEST)

def attention_scores(queries, key_nope, key_rope, allowed):
    score_scale = (NOPE + ROPE) ** (-0.5)
    raw_scores = product('qhd,khd->hqk', queries[..., :NOPE], key_nope)
    raw_scores = raw_scores + product('qhd,kd->hqk', queries[..., NOPE:], key_rope)
    return jnp.where(allowed[None, :, :], raw_scores * score_scale, -jnp.inf)

def attention_forward(x_rows, doc_row, attn_gain, query_weight, kv_down_weight, kv_gain, kv_up_weight):
    rows_count = x_rows.shape[0]
    cosine, sine_table = rope_tables(doc_positions(doc_row))
    index_row = jnp.arange(rows_count, dtype=jnp.int32)
    allowed = (doc_row[:, None] == doc_row[None, :]) & (index_row[None, :] <= index_row[:, None])
    x_float = x_rows.astype(jnp.float32)
    scale_in = inv_rms(x_float)
    x_norm = (x_float * scale_in * attn_gain).astype(jnp.bfloat16)
    query_raw = jnp.dot(x_norm, query_weight, preferred_element_type=jnp.float32).reshape(rows_count, HEADS, NOPE + ROPE)
    queries = jnp.concatenate([query_raw[..., :NOPE], rotate(query_raw[..., NOPE:], cosine[:, None, :], sine_table[:, None, :])], axis=-1).astype(jnp.bfloat16)
    latent_raw = jnp.dot(x_norm, kv_down_weight, preferred_element_type=jnp.float32)
    compressed = latent_raw[:, :KV_RANK]
    scale_kv = inv_rms(compressed)
    latent = jnp.concatenate([compressed * scale_kv * kv_gain, rotate(latent_raw[:, KV_RANK:], cosine, sine_table)], axis=-1).astype(jnp.bfloat16)
    key_rope = latent[:, KV_RANK:]
    expanded = jnp.dot(latent[:, :KV_RANK], kv_up_weight, preferred_element_type=jnp.float32).astype(jnp.bfloat16).reshape(rows_count, HEADS, NOPE + VDIM)
    key_nope = expanded[..., :NOPE]
    values_all = expanded[..., NOPE:]
    scores = attention_scores(queries, key_nope, key_rope, allowed)
    row_max = lax.optimization_barrier(jnp.max(scores, axis=-1, keepdims=True))
    lse_rows = row_max + jnp.log(lax.optimization_barrier(jnp.sum(jnp.exp(scores - row_max), axis=-1, keepdims=True)))
    probs_full = jnp.exp(scores - lse_rows)
    probs_low = probs_full.astype(jnp.bfloat16)
    attended = product('hqk,khd->qhd', probs_low, values_all).astype(jnp.bfloat16).reshape(rows_count, HEADS * VDIM)
    return (x_float, scale_in, x_norm, queries, compressed, scale_kv, latent, key_nope, values_all, key_rope, probs_full, probs_low, attended, cosine, sine_table)

def attention_backward(x_rows, doc_row, resid_grad, attn_gain, query_weight, kv_down_weight, kv_gain, kv_up_weight, out_weight):
    x_float, scale_in, x_norm, queries, compressed, scale_kv, latent, key_nope, values_all, key_rope, probs_full, probs_low, attended, cosine, sine_table = attention_forward(x_rows, doc_row, attn_gain, query_weight, kv_down_weight, kv_gain, kv_up_weight)
    rows_count = x_rows.shape[0]
    score_scale = (NOPE + ROPE) ** (-0.5)
    resid_low = resid_grad.astype(jnp.bfloat16)
    out_weight_grad = jnp.dot(attended.T, resid_low, preferred_element_type=jnp.float32)
    attended_grad = jnp.dot(resid_low, out_weight.T, preferred_element_type=jnp.float32).astype(jnp.bfloat16).reshape(rows_count, HEADS, VDIM)
    values_grad = product('hqk,qhd->khd', probs_low, attended_grad)
    probs_grad = product('qhd,khd->hqk', attended_grad, values_all)
    delta_rows = lax.optimization_barrier(jnp.sum(probs_full * probs_grad, axis=-1, keepdims=True))
    score_grad = (probs_full * (probs_grad - delta_rows) * score_scale).astype(jnp.bfloat16)
    query_nope_grad = product('hqk,khd->qhd', score_grad, key_nope)
    query_rope_grad = product('hqk,kd->qhd', score_grad, key_rope)
    key_nope_grad = product('hqk,qhd->khd', score_grad, queries[..., :NOPE])
    rope_grad = product('hqk,qhd->kd', score_grad, queries[..., NOPE:])
    key_grad = jnp.concatenate([key_nope_grad, values_grad], axis=-1).reshape(rows_count, HEADS * (NOPE + VDIM)).astype(jnp.bfloat16)
    kv_up_weight_grad = jnp.dot(latent[:, :KV_RANK].T, key_grad, preferred_element_type=jnp.float32)
    latent_back = jnp.dot(key_grad, kv_up_weight.T, preferred_element_type=jnp.float32)
    compressed_grad, kv_gain_grad = norm_back(latent_back, compressed, scale_kv, kv_gain)
    latent_grad = jnp.concatenate([compressed_grad, unrotate(rope_grad, cosine, sine_table)], axis=-1).astype(jnp.bfloat16)
    kv_down_weight_grad = jnp.dot(x_norm.T, latent_grad, preferred_element_type=jnp.float32)
    query_grad = jnp.concatenate([query_nope_grad, unrotate(query_rope_grad, cosine[:, None, :], sine_table[:, None, :])], axis=-1).reshape(rows_count, HEADS * (NOPE + ROPE)).astype(jnp.bfloat16)
    query_weight_grad = jnp.dot(x_norm.T, query_grad, preferred_element_type=jnp.float32)
    norm_grad = jnp.dot(latent_grad, kv_down_weight.T, preferred_element_type=jnp.float32) + jnp.dot(query_grad, query_weight.T, preferred_element_type=jnp.float32)
    input_part, attn_gain_grad = norm_back(norm_grad, x_float, scale_in, attn_gain)
    return (resid_grad + input_part, (attn_gain_grad, query_weight_grad, kv_down_weight_grad, kv_gain_grad, kv_up_weight_grad, out_weight_grad))

def reference(block_in, cotangent, doc_ids, routes, attn_gain, query_weight, kv_down_weight, kv_gain, kv_up_weight, out_weight, ffn_gain, router_weight, shared_in, shared_down, expert_in, expert_down):
    tokens_all = block_in.shape[0]
    groups_all = doc_ids.shape[0]
    x_groups = block_in.reshape(groups_all, GROUP_TOK, D)

    def forward_group(inputs_g):
        x_rows, doc_row = inputs_g
        pieces = attention_forward(x_rows, doc_row, attn_gain, query_weight, kv_down_weight, kv_gain, kv_up_weight)
        return pieces[0] + jnp.dot(pieces[12], out_weight, preferred_element_type=jnp.float32)
    resid = lax.map(forward_group, (x_groups, doc_ids)).reshape(tokens_all, D)
    scale_ffn = inv_rms(resid)
    h_norm = (resid * scale_ffn * ffn_gain).astype(jnp.bfloat16)
    logits = jnp.dot(h_norm, router_weight, preferred_element_type=jnp.float32)
    expert_ids = jnp.arange(EXPERTS, dtype=jnp.int32)
    route_hot = (routes[:, :, None] == expert_ids[None, None, :]).astype(jnp.float32)
    chosen = lax.optimization_barrier(jnp.sum(route_hot * logits[:, None, :], axis=-1))
    route_weights = jax.nn.softmax(chosen, axis=-1)
    shared_pre = jnp.dot(h_norm, shared_in, preferred_element_type=jnp.float32)
    shared_act, shared_slope = silu_parts(shared_pre[:, :SH_FF])
    shared_mid = (shared_act * shared_pre[:, SH_FF:]).astype(jnp.bfloat16)
    shared_out = jnp.dot(shared_mid, shared_down, preferred_element_type=jnp.float32)
    devices_all = tokens_all // TOK_DEV
    per_dev = TOK_DEV * TOP
    route_dev = routes.reshape(devices_all, per_dev)
    dev_hot = (route_dev[:, :, None] == expert_ids[None, None, :]).astype(jnp.int32)
    slot_rank = lax.optimization_barrier(jnp.sum((jnp.cumsum(dev_hot, axis=1) - 1) * dev_hot, axis=2))
    slot_index = route_dev * CAP + slot_rank
    device_ids = jnp.arange(devices_all, dtype=jnp.int32)
    flat_ids = device_ids[:, None] * per_dev + jnp.arange(per_dev, dtype=jnp.int32)[None, :]
    sentinel = tokens_all * TOP
    slot_table = jnp.full((devices_all, EXPERTS * CAP), sentinel, dtype=jnp.int32).at[device_ids[:, None], slot_index].set(flat_ids)
    slot_table = slot_table.reshape(devices_all, EXPERTS, CAP).transpose(1, 0, 2).reshape(EXPERTS, devices_all * CAP)
    cot_float = cotangent.astype(jnp.float32)
    norm_ext = jnp.concatenate([h_norm, jnp.zeros((1, D), jnp.bfloat16)], axis=0)
    cot_ext = jnp.concatenate([cot_float, jnp.zeros((1, D), jnp.float32)], axis=0)
    weights_ext = jnp.concatenate([route_weights.reshape(-1), jnp.zeros((1,), jnp.float32)], axis=0)

    def expert_step(totals, inputs_j):
        routed_acc, back_acc, weight_acc = totals
        in_rows, down_rows, flat_rows = inputs_j
        token_rows = flat_rows // TOP
        rows_in = norm_ext[token_rows]
        gate_pre = jnp.dot(rows_in, in_rows[:D], preferred_element_type=jnp.float32)
        up_pre = jnp.dot(rows_in, in_rows[D:], preferred_element_type=jnp.float32)
        gate_act, gate_slope = silu_parts(gate_pre)
        expert_mid = (gate_act * up_pre).astype(jnp.bfloat16)
        result_low = jnp.dot(expert_mid, down_rows.T, preferred_element_type=jnp.float32).astype(jnp.bfloat16)
        result_float = lax.optimization_barrier(result_low).astype(jnp.float32)
        weight_rows = weights_ext[flat_rows]
        cot_rows = cot_ext[token_rows]
        routed_acc = routed_acc.at[token_rows].add(weight_rows[:, None] * result_float)
        weight_acc = weight_acc.at[flat_rows].add(lax.optimization_barrier(jnp.sum(cot_rows * result_float, axis=-1)))
        grad_rows = (weight_rows[:, None] * cot_rows).astype(jnp.bfloat16)
        down_grad = jnp.dot(grad_rows.T, expert_mid, preferred_element_type=jnp.float32)
        mid_grad = jnp.dot(grad_rows, down_rows, preferred_element_type=jnp.float32)
        gate_grad = (mid_grad * up_pre * gate_slope).astype(jnp.bfloat16)
        up_grad = (mid_grad * gate_act).astype(jnp.bfloat16)
        in_grad = jnp.concatenate([jnp.dot(rows_in.T, gate_grad, preferred_element_type=jnp.float32), jnp.dot(rows_in.T, up_grad, preferred_element_type=jnp.float32)], axis=0)
        back_float = jnp.dot(gate_grad, in_rows[:D].T, preferred_element_type=jnp.float32) + jnp.dot(up_grad, in_rows[D:].T, preferred_element_type=jnp.float32)
        back_round = lax.optimization_barrier(back_float.astype(jnp.bfloat16)).astype(jnp.float32)
        back_acc = back_acc.at[token_rows].add(back_round)
        return ((routed_acc, back_acc, weight_acc), (in_grad, down_grad))
    start_totals = (jnp.zeros((tokens_all + 1, D), jnp.float32), jnp.zeros((tokens_all + 1, D), jnp.float32), jnp.zeros((sentinel + 1,), jnp.float32))
    (routed_acc, back_acc, weight_acc), (in_grads, down_grads) = lax.scan(expert_step, start_totals, (expert_in, expert_down, slot_table))
    block_out = resid + shared_out + routed_acc[:tokens_all]
    shared_down_grad = jnp.dot(shared_mid.T, cotangent, preferred_element_type=jnp.float32)
    mid_back = jnp.dot(cotangent, shared_down.T, preferred_element_type=jnp.float32)
    shared_pre_grad = jnp.concatenate([mid_back * shared_pre[:, SH_FF:] * shared_slope, mid_back * shared_act], axis=-1).astype(jnp.bfloat16)
    shared_in_grad = jnp.dot(h_norm.T, shared_pre_grad, preferred_element_type=jnp.float32)
    hidden_grad = jnp.dot(shared_pre_grad, shared_in.T, preferred_element_type=jnp.float32) + back_acc[:tokens_all]
    weight_grad = weight_acc[:sentinel].reshape(tokens_all, TOP)
    chosen_grad = route_weights * (weight_grad - lax.optimization_barrier(jnp.sum(route_weights * weight_grad, axis=-1, keepdims=True)))
    logit_grad = lax.optimization_barrier(jnp.sum(route_hot * chosen_grad[:, :, None], axis=1)).astype(jnp.bfloat16)
    router_grad = jnp.dot(h_norm.T, logit_grad, preferred_element_type=jnp.float32)
    hidden_grad = hidden_grad + jnp.dot(logit_grad, router_weight.T, preferred_element_type=jnp.float32)
    resid_part, ffn_gain_grad = norm_back(hidden_grad, resid, scale_ffn, ffn_gain)
    resid_grad = cot_float + resid_part
    zero_grads = (jnp.zeros(attn_gain.shape, jnp.float32), jnp.zeros(query_weight.shape, jnp.float32), jnp.zeros(kv_down_weight.shape, jnp.float32), jnp.zeros(kv_gain.shape, jnp.float32), jnp.zeros(kv_up_weight.shape, jnp.float32), jnp.zeros(out_weight.shape, jnp.float32))

    def backward_group(totals, inputs_g):
        x_rows, doc_row, grad_rows = inputs_g
        x_grad_rows, terms = attention_backward(x_rows, doc_row, grad_rows, attn_gain, query_weight, kv_down_weight, kv_gain, kv_up_weight, out_weight)
        return (jax.tree.map(jnp.add, totals, terms), x_grad_rows)
    attn_totals, input_grad = lax.scan(backward_group, zero_grads, (x_groups, doc_ids, resid_grad.reshape(groups_all, GROUP_TOK, D)))
    input_grad = input_grad.reshape(tokens_all, D)
    return (block_out, input_grad, attn_totals[0], attn_totals[1], attn_totals[2], attn_totals[3], attn_totals[4], attn_totals[5], ffn_gain_grad, router_grad, shared_in_grad, shared_down_grad, in_grads, down_grads)
```

```python
import jax
import jax.numpy as jnp
from jax import lax
from jax.sharding import PartitionSpec as P

D = 2048
HEADS = 16
NOPE = 128
ROPE = 64
VDIM = 128
QK = NOPE + ROPE
KV_RANK = 512
SH_FF = 2816
EXP_DEV = 2
FF_PAD = 896

EPS = 1e-06
ROPE_BASE = 10000.0
BOTH = ("expert", "shard")
bf16 = jnp.bfloat16
f32 = jnp.float32


def dot(a, b, dims):
    return lax.dot_general(a, b, (dims, ((), ())), preferred_element_type=f32)


def mm(a, b):
    return dot(a, b, ((1,), (0,)))


def mm_tn(a, b):
    return dot(a, b, ((0,), (0,)))


def mm_nt(a, b):
    return dot(a, b, ((1,), (1,)))


def inv_rms(values):
    return lax.rsqrt(jnp.mean(values * values, axis=-1, keepdims=True) + EPS)


def norm_back(grad_out, values, inv_scale, gain_row):
    scaled = grad_out * gain_row
    grad_in = inv_scale * scaled - values * inv_scale**3 * jnp.mean(
        scaled * values, axis=-1, keepdims=True
    )
    grad_gain = jnp.sum(grad_out * values * inv_scale, axis=0)
    return (grad_in, grad_gain)


def rope_tables(doc_row):
    count = doc_row.shape[0]
    index = jnp.arange(count, dtype=jnp.int32)
    before = (doc_row[:, None] == doc_row[None, :]) & (index[None, :] < index[:, None])
    positions = jnp.sum(before.astype(f32), axis=1)
    half = ROPE // 2
    frequency = ROPE_BASE ** (-jnp.arange(half, dtype=f32) / half)
    angles = positions[:, None] * frequency[None, :]
    return (jnp.cos(angles), jnp.sin(angles))


def rotate(values, cosine, sine):
    half = cosine.shape[-1]
    a, b = values[..., :half], values[..., half:]
    return jnp.concatenate([a * cosine - b * sine, b * cosine + a * sine], axis=-1)


def unrotate(values, cosine, sine):
    return rotate(values, cosine, -sine)


def swap(value, bit, count):
    return lax.ppermute(value, "expert", [(i, i ^ bit) for i in range(count)])


def plane_gather(v, count):
    if count != 8:
        return lax.all_gather(v, "expert", axis=0)
    half = v.shape[-1] // 2
    vx, vy = swap(v, 2, count), swap(v, 4, count)
    vd = jnp.concatenate(
        [swap(vx[..., :half], 4, count), swap(vy[..., half:], 2, count)], axis=-1
    )
    parts = []
    for part in (v, vx, vy, vd):
        parts += [part, swap(part, 1, count)]
    return jnp.stack(parts)


def plane_reduce(p, count):
    if count != 8:
        return lax.psum_scatter(p, "expert", scatter_dimension=0, tiled=False)
    kind = p.dtype
    half = p.shape[-1] // 2
    r = [p[j].astype(f32) + swap(p[j + 1], 1, count).astype(f32) for j in (0, 2, 4, 6)]
    low = r[3].astype(kind)
    r1a = r[1][..., half:] + swap(low[..., half:], 4, count).astype(f32)
    r2a = r[2][..., :half] + swap(low[..., :half], 2, count).astype(f32)
    r1 = jnp.concatenate([r[1][..., :half], r1a], axis=-1).astype(kind)
    r2 = jnp.concatenate([r2a, r[2][..., half:]], axis=-1).astype(kind)
    return r[0] + swap(r1, 2, count).astype(f32) + swap(r2, 4, count).astype(f32)


def local(
    block_in,
    cotangent,
    doc_ids,
    routes,
    attn_gain,
    query_weight,
    kv_down_weight,
    kv_gain,
    kv_up_weight,
    out_weight,
    ffn_gain,
    router_weight,
    shared_in,
    shared_down,
    expert_in,
    expert_down,
):
    tok = block_in.shape[0]
    E, S = lax.axis_size("expert"), lax.axis_size("shard")
    e, s = lax.axis_index("expert"), lax.axis_index("shard")
    group = tok * S
    heads = HEADS // S
    units = SH_FF // (E * S)
    experts_all = EXP_DEV * E
    ff = expert_in.shape[2]
    first = s * tok
    scale = QK ** (-0.5)

    def own(v):
        return lax.dynamic_slice_in_dim(v, first, tok, 0)

    def gather(v):
        return lax.all_gather(v, "shard", axis=0, tiled=True)

    gain_a, gain_f, gain_k = gather(attn_gain), gather(ffn_gain), gather(kv_gain)
    router = gather(router_weight)
    kv_down = gather(kv_down_weight)
    w_out = gather(out_weight)

    def columns_to_heads(w):
        rows, cols = w.shape
        parts = w.reshape(rows, S, cols // S)
        return lax.all_to_all(parts, "shard", split_axis=1, concat_axis=0, tiled=True).reshape(
            rows * S, cols // S
        )

    w_q = columns_to_heads(query_weight)
    kv_up = columns_to_heads(kv_up_weight)
    x_rows = gather(block_in)
    cot_rows = gather(cotangent)
    routes_rows = gather(routes)

    def shared_columns(w, start):
        part = lax.dynamic_slice_in_dim(w, start + e * S * units, S * units, 1)
        return columns_to_heads(part)

    sh_gate, sh_up = shared_columns(shared_in, 0), shared_columns(shared_in, SH_FF)
    rows_here = shared_down.shape[0]
    sends = []
    for j in range(S):
        at = (e * S + j) * units - s * rows_here
        sends.append(lax.dynamic_slice_in_dim(shared_down, jnp.clip(at, 0, rows_here - units), units, 0))
    got = lax.all_to_all(jnp.stack(sends), "shard", split_axis=0, concat_axis=0, tiled=True)
    sh_down = lax.dynamic_index_in_dim(got, (e * S + s) * units // rows_here, 0, keepdims=False)

    pad = jnp.zeros((D, FF_PAD - EXP_DEV * ff - units), bf16)
    w_in = jnp.concatenate(
        [expert_in[0, :D], expert_in[1, :D], sh_gate, pad, expert_in[0, D:], expert_in[1, D:], sh_up, pad],
        axis=1,
    )
    w_down = jnp.concatenate([expert_down[0], expert_down[1], sh_down.T, pad], axis=1)

    doc_row = doc_ids[0]
    cosine, sine = rope_tables(doc_row)
    index = jnp.arange(group, dtype=jnp.int32)
    allowed = (doc_row[:, None] == doc_row[None, :]) & (index[None, :] <= index[:, None])
    x_float = x_rows.astype(f32)
    scale_in = inv_rms(x_float)
    x_norm = (x_float * scale_in * gain_a).astype(bf16)
    query_raw = mm(x_norm, w_q).reshape(group, heads, QK)
    queries = jnp.concatenate(
        [
            query_raw[..., :NOPE],
            rotate(query_raw[..., NOPE:], cosine[:, None, :], sine[:, None, :]),
        ],
        axis=-1,
    ).astype(bf16)
    latent_raw = mm(x_norm, kv_down)
    compressed = latent_raw[:, :KV_RANK]
    scale_kv = inv_rms(compressed)
    latent = (compressed * scale_kv * gain_k).astype(bf16)
    key_rope = rotate(latent_raw[:, KV_RANK:], cosine, sine).astype(bf16)
    expanded = mm(latent, kv_up).astype(bf16).reshape(group, heads, NOPE + VDIM)
    keys = jnp.concatenate(
        [expanded[..., :NOPE], jnp.broadcast_to(key_rope[:, None, :], (group, heads, ROPE))], axis=-1
    )
    values = expanded[..., NOPE:]
    scores = jnp.einsum("qhd,khd->hqk", queries, keys, preferred_element_type=f32)
    scores = jnp.where(allowed[None], scores * scale, -jnp.inf)
    row_max = jnp.max(scores, axis=-1, keepdims=True)
    lse = row_max + jnp.log(jnp.sum(jnp.exp(scores - row_max), axis=-1, keepdims=True))
    probs = jnp.exp(scores - lse)
    probs_low = probs.astype(bf16)
    attended = (
        jnp.einsum("hqk,khd->qhd", probs_low, values, preferred_element_type=f32)
        .astype(bf16)
        .reshape(group, heads * VDIM)
    )
    attended_all = lax.all_gather(attended, "shard", axis=1, tiled=True)

    resid = x_float + mm(attended_all, w_out)
    scale_ffn = inv_rms(resid)
    h_norm = (resid * scale_ffn * gain_f).astype(bf16)
    logits = mm(h_norm, router)
    expert_ids = jnp.arange(experts_all, dtype=jnp.int32)
    named = jnp.any(routes_rows[:, :, None] == expert_ids[None, None, :], axis=1)
    masked = jnp.where(named, logits, -jnp.inf)
    top = jnp.exp(masked - jnp.max(masked, axis=-1, keepdims=True))
    route_w = top / jnp.sum(top, axis=-1, keepdims=True)

    unit_at = slice(EXP_DEV * ff, EXP_DEV * ff + units)
    spot = (expert_ids[:, None] == (e * EXP_DEV + jnp.arange(EXP_DEV, dtype=jnp.int32))[None, :]).astype(f32)

    def hidden_units(h_rows, cot_part, w_rows):
        part = h_rows.shape[0]
        count = E * part
        h_all = plane_gather(h_rows, E).reshape(count, D)
        cot_all = plane_gather(cot_part, E).reshape(count, D)
        w_own = lax.dynamic_slice_in_dim(plane_gather(w_rows.T, E), e * EXP_DEV, EXP_DEV, 1)
        cols = w_own.transpose(0, 2, 1).reshape(count, EXP_DEV)
        weight = jnp.concatenate(
            [
                jnp.broadcast_to(cols[:, :1], (count, ff)),
                jnp.broadcast_to(cols[:, 1:], (count, ff)),
                jnp.ones((count, FF_PAD - EXP_DEV * ff), f32),
            ],
            axis=1,
        )
        pre = mm(h_all, w_in)
        gate_pre, up_pre = pre[:, :FF_PAD], pre[:, FF_PAD:]
        mid_grad = mm(cot_all, w_down)
        sigmoid = jax.nn.sigmoid(gate_pre)
        act = gate_pre * sigmoid
        slope = sigmoid * (1.0 + gate_pre * (1.0 - sigmoid))
        mid = act * up_pre
        mid_low = (weight * mid).astype(bf16)
        weighted = weight * mid_grad
        gate_grad = (weighted * up_pre * slope).astype(bf16)
        up_grad = (weighted * act).astype(bf16)
        product = mid * mid_grad
        wg = jnp.stack([jnp.sum(product[:, k * ff : (k + 1) * ff], axis=1) for k in range(EXP_DEV)])
        out_part = mm_nt(mid_low, w_down).astype(bf16).reshape(E, part, D)
        pre_grad = jnp.concatenate([gate_grad, up_grad], axis=1)
        back_part = mm_nt(pre_grad, w_in).astype(bf16).reshape(E, part, D)
        in_grad = jnp.stack(
            [
                jnp.concatenate([mm_tn(h_all, g[:, k * ff : (k + 1) * ff]) for g in (gate_grad, up_grad)], axis=0)
                for k in range(EXP_DEV)
            ]
        )
        down_grad = jnp.stack([mm_tn(cot_all, mid_low[:, k * ff : (k + 1) * ff]) for k in range(EXP_DEV)])
        sh_down_grad = mm_tn(mid_low[:, unit_at], cot_all)
        sh_in_grad = mm_tn(h_all, jnp.concatenate([gate_grad[:, unit_at], up_grad[:, unit_at]], axis=1))
        wg = wg.reshape(EXP_DEV, E, part).transpose(1, 0, 2)
        wg_full = jnp.sum(spot[None, :, :, None] * wg[:, None, :, :], axis=2)
        sums = (plane_reduce(out_part, E), plane_reduce(back_part, E), plane_reduce(wg_full, E).T)
        return ((in_grad, down_grad, sh_down_grad, sh_in_grad), sums)

    pieces = max(1, E // 8)
    if pieces == 1:
        grads, sums = hidden_units(h_norm, cot_rows, route_w)
    else:
        rows_in = [v.reshape(pieces, -1, v.shape[-1]) for v in (h_norm, cot_rows, route_w)]

        def one(total, rows):
            made, sums = hidden_units(*rows)
            return (jax.tree.map(jnp.add, total, made), sums)

        zeros = (
            jnp.zeros(expert_in.shape, f32),
            jnp.zeros(expert_down.shape, f32),
            jnp.zeros((units, D), f32),
            jnp.zeros((D, 2 * units), f32),
        )
        grads, sums = lax.scan(one, zeros, tuple(rows_in))
        sums = [v.reshape(-1, v.shape[-1]) for v in sums]
    expert_in_grad, expert_down_grad, shared_down_grad, sh_in_grad = grads
    sh_in_grad = lax.all_to_all(
        sh_in_grad.reshape(E * S, D // (E * S), 2 * units), BOTH, split_axis=0, concat_axis=0, tiled=True
    )
    shared_in_grad = (
        sh_in_grad.reshape(E * S, D // (E * S), 2, units).transpose(1, 2, 0, 3).reshape(D // (E * S), 2 * SH_FF)
    )
    out_sum, back_sum, wg_sum = sums

    def owners_sum(part):
        return lax.psum_scatter(part, "shard", scatter_dimension=0, tiled=True).astype(f32)

    routed = owners_sum(out_sum.astype(bf16))
    hidden_grad = owners_sum(back_sum.astype(bf16))
    weight_grad = owners_sum(wg_sum)

    resid_own, h_own, w_tok, scale_own = own(resid), own(h_norm), own(route_w), own(scale_ffn)
    block_out = resid_own + routed
    logit_grad = (w_tok * (weight_grad - jnp.sum(w_tok * weight_grad, axis=-1, keepdims=True))).astype(bf16)
    router_grad = mm_tn(h_own, logit_grad)
    hidden_grad = hidden_grad + mm_nt(logit_grad, router)
    resid_part, ffn_gain_grad = norm_back(hidden_grad, resid_own, scale_own, gain_f)
    resid_grad = cotangent.astype(f32) + resid_part
    resid_low = resid_grad.astype(bf16)

    attended_grad = mm_nt(resid_low, w_out).astype(bf16)
    both = jnp.concatenate([attended_grad, resid_low], axis=1).reshape(tok, 2, S, D // S)
    both = lax.all_to_all(both, "shard", split_axis=2, concat_axis=0, tiled=True).reshape(group, 2, D // S)
    att_grad = both[:, 0].reshape(group, heads, VDIM)
    resid_cols = both[:, 1]
    out_grad = mm_tn(attended_all, resid_cols)

    values_grad = jnp.einsum("hqk,qhd->khd", probs_low, att_grad, preferred_element_type=f32)
    probs_grad = jnp.einsum("qhd,khd->hqk", att_grad, values, preferred_element_type=f32)
    delta = jnp.sum(probs * probs_grad, axis=-1, keepdims=True)
    score_grad = (probs * (probs_grad - delta) * scale).astype(bf16)
    q_grad = jnp.einsum("hqk,khd->qhd", score_grad, keys, preferred_element_type=f32)
    k_grad = jnp.einsum("hqk,qhd->khd", score_grad, queries, preferred_element_type=f32)
    rope_part = jnp.sum(k_grad[..., NOPE:], axis=1)
    key_grad = (
        jnp.concatenate([k_grad[..., :NOPE], values_grad], axis=-1)
        .reshape(group, heads * (NOPE + VDIM))
        .astype(bf16)
    )
    query_grad = (
        jnp.concatenate(
            [q_grad[..., :NOPE], unrotate(q_grad[..., NOPE:], cosine[:, None, :], sine[:, None, :])], axis=-1
        )
        .reshape(group, heads * QK)
        .astype(bf16)
    )
    latent_part = jnp.concatenate([mm_nt(key_grad, kv_up), rope_part], axis=1)
    norm_part = mm_nt(query_grad, w_q)
    latent_back = lax.psum_scatter(latent_part.astype(bf16), "shard", scatter_dimension=0, tiled=True).astype(f32)
    norm_sum = lax.psum_scatter(norm_part.astype(bf16), "shard", scatter_dimension=0, tiled=True).astype(f32)
    compressed_grad, kv_gain_grad = norm_back(latent_back[:, :KV_RANK], own(compressed), own(scale_kv), gain_k)
    latent_grad = jnp.concatenate(
        [compressed_grad, unrotate(latent_back[:, KV_RANK:], own(cosine), own(sine))], axis=1
    ).astype(bf16)
    norm_grad = norm_sum + mm_nt(latent_grad, kv_down)
    input_part, attn_gain_grad = norm_back(norm_grad, own(x_float), own(scale_in), gain_a)
    input_grad = resid_grad + input_part

    q_w_grad = mm_tn(x_norm, query_grad)
    kv_up_grad = mm_tn(latent, key_grad)
    latent_grad_rows = gather(latent_grad)
    x_cols = lax.dynamic_slice_in_dim(x_norm, s * (D // S), D // S, 1)
    kv_down_grad = mm_tn(x_cols, latent_grad_rows)

    def scatter_columns(g):
        rows, cols = g.shape
        mine = lax.psum_scatter(g.astype(bf16), "expert", scatter_dimension=0, tiled=True)
        mine = lax.all_to_all(
            mine.reshape(S, rows // (E * S), cols), "shard", split_axis=0, concat_axis=0, tiled=True
        )
        return mine.transpose(1, 0, 2).reshape(rows // (E * S), S * cols).astype(f32)

    query_weight_grad = scatter_columns(q_w_grad)
    kv_up_weight_grad = scatter_columns(kv_up_grad)
    out_weight_grad = scatter_columns(out_grad)
    rows = D // (E * S)
    mine = lax.psum_scatter(kv_down_grad.astype(bf16), "expert", scatter_dimension=0, tiled=True)
    pairs = [(ee * S + ss, E * ss + ee) for ee in range(E) for ss in range(S)]
    kv_down_weight_grad = lax.ppermute(mine, BOTH, pairs).astype(f32)

    small = jnp.concatenate([router_grad, ffn_gain_grad[:, None], attn_gain_grad[:, None]], axis=1)
    small = lax.psum_scatter(small, BOTH, scatter_dimension=0, tiled=True)
    kv_gain_grad = lax.psum_scatter(kv_gain_grad, BOTH, scatter_dimension=0, tiled=True)
    return (
        block_out,
        input_grad,
        small[:, experts_all + 1],
        query_weight_grad,
        kv_down_weight_grad,
        kv_gain_grad,
        kv_up_weight_grad,
        out_weight_grad,
        small[:, experts_all],
        small[:, :experts_all],
        shared_in_grad,
        shared_down_grad,
        expert_in_grad,
        expert_down_grad,
    )


def solution(mesh):
    tokens = P(BOTH, None)
    shard = P("shard", None)
    in_specs = (
        tokens,
        tokens,
        P("expert", None),
        tokens,
        P("shard"),
        shard,
        shard,
        P("shard"),
        shard,
        shard,
        P("shard"),
        shard,
        shard,
        shard,
        P("expert", None, "shard"),
        P("expert", None, "shard"),
    )
    out_specs = (
        tokens,
        tokens,
        P(BOTH),
        tokens,
        tokens,
        P(BOTH),
        tokens,
        tokens,
        P(BOTH),
        tokens,
        tokens,
        tokens,
        P("expert", None, "shard"),
        P("expert", None, "shard"),
    )
    return jax.shard_map(local, mesh=mesh, in_specs=in_specs, out_specs=out_specs, check_vma=False)
```

```python
import functools

import jax
import jax.numpy as jnp
from jax import lax
from jax.experimental import pallas as pl
from jax.experimental.pallas import tpu as pltpu
from jax.sharding import PartitionSpec as P

D = 2048
HEADS = 16
NOPE = 128
ROPE = 64
VDIM = 128
QK = NOPE + ROPE
KV_RANK = 512
SH_FF = 2816
EXP_DEV = 2
FF_PAD = 896

EPS = 1e-06
ROPE_BASE = 10000.0
BOTH = ("expert", "shard")
bf16 = jnp.bfloat16
f32 = jnp.float32


def dot(a, b, dims):
    return lax.dot_general(a, b, (dims, ((), ())), preferred_element_type=f32)


def mm(a, b):
    return dot(a, b, ((1,), (0,)))


def mm_tn(a, b):
    return dot(a, b, ((0,), (0,)))


def mm_nt(a, b):
    return dot(a, b, ((1,), (1,)))


def inv_rms(values):
    return lax.rsqrt(jnp.mean(values * values, axis=-1, keepdims=True) + EPS)


def norm_back(grad_out, values, inv_scale, gain_row):
    scaled = grad_out * gain_row
    grad_in = inv_scale * scaled - values * inv_scale**3 * jnp.mean(
        scaled * values, axis=-1, keepdims=True
    )
    grad_gain = jnp.sum(grad_out * values * inv_scale, axis=0)
    return (grad_in, grad_gain)


def rope_tables(doc_row):
    count = doc_row.shape[0]
    index = jnp.arange(count, dtype=jnp.int32)
    before = (doc_row[:, None] == doc_row[None, :]) & (index[None, :] < index[:, None])
    positions = jnp.sum(before.astype(f32), axis=1)
    half = ROPE // 2
    frequency = ROPE_BASE ** (-jnp.arange(half, dtype=f32) / half)
    angles = positions[:, None] * frequency[None, :]
    return (jnp.cos(angles), jnp.sin(angles))


def rotate(values, cosine, sine):
    half = cosine.shape[-1]
    a, b = values[..., :half], values[..., half:]
    return jnp.concatenate([a * cosine - b * sine, b * cosine + a * sine], axis=-1)


def unrotate(values, cosine, sine):
    return rotate(values, cosine, -sine)


def flip(index, bit):
    return index + bit - 2 * bit * ((index // bit) % 2)


ANY = pl.BlockSpec(memory_space=pl.ANY)
MESH = pl.DeviceIdType.MESH


def remote(src, dst, send, recv, **where):
    return pltpu.make_async_remote_copy(
        src_ref=src, dst_ref=dst, send_sem=send, recv_sem=recv, device_id=where, device_id_type=MESH
    )


def greet(peers):
    barrier = pltpu.get_barrier_semaphore()
    for where in peers:
        pl.semaphore_signal(barrier, inc=1, device_id=where, device_id_type=MESH)
    pl.semaphore_wait(barrier, len(peers))


def exchange_views(kind, src, dst, S):
    if kind == "rows":
        r = src.shape[0]
        return (lambda t: src), (lambda q: dst.at[pl.ds(q * r, r)])
    if kind == "cols":
        c = src.shape[1]
        return (lambda t: src), (lambda q: dst.at[:, pl.ds(q * c, c)])
    if kind == "cols_to_rows":
        r, c = src.shape[0], src.shape[1] // S
        return (lambda t: src.at[:, pl.ds(t * c, c)]), (lambda q: dst.at[pl.ds(q * r, r)])
    if kind == "rows_to_cols":
        r, c = src.shape[0] // S, src.shape[1]
        return (lambda t: src.at[pl.ds(t * r, r)]), (lambda q: dst.at[:, pl.ds(q * c, c)])
    r = src.shape[0] // S
    return (lambda t: src.at[pl.ds(t * r, r)]), (lambda q: dst.at[pl.ds(q * r, r)])


def exchange_shape(kind, a, S):
    r, c = a.shape
    return {
        "rows": (S * r, c),
        "cols": (r, S * c),
        "cols_to_rows": (S * r, c // S),
        "rows_to_cols": (r // S, S * c),
        "blocks": (r, c),
    }[kind]


def shard_exchange(ident, S, *items):
    count = len(items)

    def kernel(*refs):
        ins, outs = refs[:count], refs[count : 2 * count]
        send, recv, here = refs[2 * count :]
        me = lax.axis_index("shard")
        greet([{"shard": lax.rem(me + k, S)} for k in range(1, S)])
        waits = []
        for i, (kind, _) in enumerate(items):
            out_of, into = exchange_views(kind, ins[i], outs[i], S)
            for k in range(1, S):
                to = lax.rem(me + k, S)
                waits.append(remote(out_of(to), into(me), send.at[i, k], recv.at[i, k], shard=to))
                waits[-1].start()
            waits.append(pltpu.make_async_copy(out_of(me), into(me), here.at[i]))
            waits[-1].start()
        for copy in waits:
            copy.wait()

    return pl.pallas_call(
        kernel,
        out_shape=[jax.ShapeDtypeStruct(exchange_shape(kind, a, S), a.dtype) for kind, a in items],
        in_specs=[ANY] * count,
        out_specs=[ANY] * count,
        scratch_shapes=[
            pltpu.SemaphoreType.DMA((count, S)),
            pltpu.SemaphoreType.DMA((count, S)),
            pltpu.SemaphoreType.DMA((count,)),
        ],
        compiler_params=pltpu.CompilerParams(collective_id=ident, has_side_effects=True),
    )(*[a for _, a in items])


def fetch_weights(ident, E, S, x, small, weights):
    chips = E // 2
    shaped = []
    for w, split in weights:
        r, c = w.shape
        shaped.append((w.reshape(chips, 2, r // E, c), c // S if split else c))
    count = len(weights)

    def kernel(*refs):
        x_ref, s_ref = refs[:2]
        w_refs = refs[2 : 2 + count]
        xo_ref, so_ref = refs[2 + count : 4 + count]
        o_refs = refs[4 + count : 4 + 2 * count]
        zs, zr, ps, pr, cs, cr, here = refs[4 + 2 * count :]
        me, e = lax.axis_index("shard"), lax.axis_index("expert")
        chip, core = e // 2, lax.rem(e, 2)
        greet(
            [{"shard": lax.rem(me + k, S)} for k in range(1, S)]
            + [{"expert": lax.rem(e + 2 * m, E)} for m in range(1, chips)]
            + [{"expert": flip(e, 1)}]
        )
        sent, got = [], []
        locals_ = []

        def z_copy(i, k, src, dst):
            copy = remote(src, dst, zs.at[i, k], zr.at[i, k], shard=lax.rem(me - k + S, S))
            copy.start()
            return copy

        def columns(i, t):
            c = shaped[i][1]
            if weights[i][1]:
                return w_refs[i].at[:, :, :, pl.ds(t * c, c)]
            return w_refs[i]

        def piece(i, t):
            c = shaped[i][1]
            if weights[i][1]:
                return w_refs[i].at[chip, core, :, pl.ds(t * c, c)]
            return w_refs[i].at[chip, core]

        z_waits = {}
        rows_x, rows_s = x_ref.shape[0], s_ref.shape[0]
        for k in range(1, S):
            to = lax.rem(me - k + S, S)
            for i in range(count):
                z_waits[i, k] = z_copy(i, k, piece(i, to), o_refs[i].at[me, chip, core])
        for k in range(1, S):
            z_waits["x", k] = z_copy(count, k, x_ref, xo_ref.at[pl.ds(me * rows_x, rows_x)])
            z_waits["s", k] = z_copy(count + 1, k, s_ref, so_ref.at[pl.ds(me * rows_s, rows_s)])
        for i in range(count):
            locals_.append(pltpu.make_async_copy(columns(i, me), o_refs[i].at[me], here.at[i]))
        locals_.append(pltpu.make_async_copy(x_ref, xo_ref.at[pl.ds(me * rows_x, rows_x)], here.at[count]))
        locals_.append(pltpu.make_async_copy(s_ref, so_ref.at[pl.ds(me * rows_s, rows_s)], here.at[count + 1]))
        for copy in locals_:
            copy.start()
        plane = []
        for k in range(1, S):
            q = lax.rem(me + k, S)
            for i in range(count):
                z_waits[i, k].wait_recv()
                at = o_refs[i].at[q, chip, core]
                for m in range(1, chips):
                    copy = remote(at, at, ps.at[i, k, m], pr.at[i, k, m], expert=lax.rem(e + 2 * m, E))
                    copy.start()
                    plane.append((i, k, m, copy))
        last = []
        for k in range(1, S):
            q = lax.rem(me + k, S)
            for i in range(count):
                for i2, k2, m, copy in plane:
                    if (i2, k2) == (i, k):
                        copy.wait_recv()
                at = o_refs[i].at[q, :, core]
                copy = remote(at, at, cs.at[i, k], cr.at[i, k], expert=flip(e, 1))
                copy.start()
                last.append(copy)
        for k in range(1, S):
            z_waits["x", k].wait_recv()
            z_waits["s", k].wait_recv()
        for copy in last:
            copy.wait()
        for copy in z_waits.values():
            copy.wait_send()
        for entry in plane:
            entry[3].wait_send()
        for copy in locals_:
            copy.wait()

    dma = pltpu.SemaphoreType.DMA
    outs = pl.pallas_call(
        kernel,
        out_shape=[jax.ShapeDtypeStruct((S * v.shape[0], v.shape[1]), v.dtype) for v in (x, small)]
        + [jax.ShapeDtypeStruct((S,) + v.shape[:3] + (c,), v.dtype) for v, c in shaped],
        in_specs=[ANY] * (2 + count),
        out_specs=[ANY] * (2 + count),
        scratch_shapes=[
            dma((count + 2, S)),
            dma((count + 2, S)),
            dma((count, S, chips)),
            dma((count, S, chips)),
            dma((count, S)),
            dma((count, S)),
            dma((count + 2,)),
        ],
        compiler_params=pltpu.CompilerParams(collective_id=ident, has_side_effects=True),
    )(x, small, *[v for v, _ in shaped])
    return list(outs[:2]) + [o.reshape(-1, o.shape[-1]) for o in outs[2:]]


def shared_rows(v, count):
    rows, halves = v.shape[0], v.shape[1] // 2
    width = -(-(count + 127) // 128) * 128

    def kernel(v_ref, o_ref, window, sems):
        first = lax.axis_index("expert") * count
        start = jnp.minimum(first // 128, (halves - width) // 128) * 128
        loads = [
            pltpu.make_async_copy(
                v_ref.at[:, pl.ds(pl.multiple_of(j * halves + start, 128), width)], window.at[j], sems.at[j]
            )
            for j in range(2)
        ]
        for copy in loads:
            copy.start()
        for j in range(2):
            loads[j].wait()
            turned = pltpu.roll(window[j].astype(f32), lax.rem(width - (first - start), width), 1)
            o_ref[j] = turned.T[:count].astype(bf16)

    return pl.pallas_call(
        kernel,
        out_shape=jax.ShapeDtypeStruct((2, count, rows), bf16),
        in_specs=[ANY],
        out_specs=pl.BlockSpec(memory_space=pltpu.VMEM),
        scratch_shapes=[pltpu.VMEM((2, rows, width), bf16), pltpu.SemaphoreType.DMA((2,))],
        compiler_params=pltpu.CompilerParams(vmem_limit_bytes=16 * 2**20),
    )(v)


def add_into(dst, rows, *terms):
    step = 16

    @pl.loop(0, rows // step)
    def _(i):
        at = pl.ds(pl.multiple_of(i * step, step), step)
        total = terms[0][at, :].astype(f32)
        for term in terms[1:]:
            total = total + term[at, :].astype(f32)
        dst[at, :] = total.astype(dst.dtype)


class PlaneSum:
    SEMS = 4 + 4 + 4 + 2 + 2 + 2 + 2

    @staticmethod
    def scratch(rows, cols):
        return [
            pltpu.VMEM((4, rows, cols), bf16),
            pltpu.VMEM((4, rows, cols), bf16),
            pltpu.VMEM((2, rows // 2, cols), bf16),
            pltpu.VMEM((2, rows, cols), bf16),
            pltpu.SemaphoreType.DMA((PlaneSum.SEMS,)),
        ]

    def __init__(self, term, mine, core, diag, side, sems, e):
        self.term, self.mine, self.core, self.diag, self.side, self.sems = term, mine, core, diag, side, sems
        self.rows = mine.shape[1]
        self.ec, self.ex, self.ey = flip(e, 1), flip(e, 2), flip(e, 4)
        self.at = [e, self.ex, self.ey, flip(self.ex, 4)]

    def start(self):
        self.loads = [pltpu.make_async_copy(self.term(i), self.mine.at[j], self.sems.at[j]) for j, i in enumerate(self.at)]
        self.cores = [
            remote(self.term(flip(i, 1)), self.core.at[j], self.sems.at[4 + j], self.sems.at[8 + j], expert=self.ec)
            for j, i in enumerate(self.at)
        ]
        for j in (3, 1, 2, 0):
            self.cores[j].start()
            self.loads[j].start()

    def send_diagonal(self):
        half = self.rows // 2
        self.loads[3].wait()
        self.cores[3].wait_recv()
        add_into(self.mine.at[3], self.rows, self.mine.at[3], self.core.at[3])
        low, high = self.mine.at[3, pl.ds(0, half)], self.mine.at[3, pl.ds(half, half)]
        self.diags = [
            remote(low, self.diag.at[0], self.sems.at[12], self.sems.at[14], expert=self.ex),
            remote(high, self.diag.at[1], self.sems.at[13], self.sems.at[15], expert=self.ey),
        ]
        for copy in self.diags:
            copy.start()

    def send_sides(self):
        half = self.rows // 2
        for j in (1, 2):
            self.loads[j].wait()
            self.cores[j].wait_recv()
        low, high = pl.ds(0, half), pl.ds(half, half)
        mine, core, diag = self.mine, self.core, self.diag
        add_into(mine.at[1, low], half, mine.at[1, low], core.at[1, low])
        add_into(mine.at[2, high], half, mine.at[2, high], core.at[2, high])
        self.diags[1].wait_recv()
        add_into(mine.at[1, high], half, mine.at[1, high], core.at[1, high], diag.at[1])
        self.sides = [remote(mine.at[1], self.side.at[0], self.sems.at[16], self.sems.at[18], expert=self.ex)]
        self.sides[0].start()
        self.diags[0].wait_recv()
        add_into(mine.at[2, low], half, mine.at[2, low], core.at[2, low], diag.at[0])
        self.sides.append(remote(mine.at[2], self.side.at[1], self.sems.at[17], self.sems.at[19], expert=self.ey))
        self.sides[1].start()

    def finish(self):
        self.loads[0].wait()
        self.cores[0].wait_recv()
        self.sides[0].wait_recv()
        self.sides[1].wait_recv()
        mine = self.mine.at[0]
        add_into(mine, self.rows, mine, self.core.at[0], self.side.at[0], self.side.at[1])
        for copy in self.cores + self.diags + self.sides:
            copy.wait_send()
        return mine


def reduce_weights(ident, E, S, chunks, extra):
    n, m = len(chunks), len(extra)
    arrays = []
    for a, _ in chunks:
        if not any(a is v for v in arrays):
            arrays.append(a)
    index = [next(i for i, v in enumerate(arrays) if v is a) for a, _ in chunks]
    u = len(arrays)

    def out_shape(a, kind):
        r, c = a.shape[-2:]
        if kind == "keep" or isinstance(kind, int):
            return (r, c)
        return exchange_shape(kind, jax.ShapeDtypeStruct((r, c), a.dtype), S)

    by_plane = any(kind == "plane" for kind, _ in extra)

    def kernel(*refs):
        ins, more = refs[:u], refs[u : u + m]
        outs, more_outs = refs[u + m : u + m + n], refs[u + m + n : u + n + 2 * m]
        scratch = refs[u + n + 2 * m : -3]
        send, recv, here = refs[-3:]
        me, e = lax.axis_index("shard"), lax.axis_index("expert")
        greet(
            [{"shard": lax.rem(me + k, S)} for k in range(1, S)]
            + [{"expert": lax.rem(e + k, E)} for k in range(1, E) if by_plane]
            + [{"expert": flip(e, bit)} for bit in (1, 2, 4) if not by_plane]
        )

        def term_of(j):
            ref, kind = ins[index[j]], chunks[j][1]
            if isinstance(kind, int):
                return lambda i: ref.at[i, lax.rem(me + kind, S)]
            return lambda i: ref.at[i]

        sums = [PlaneSum(term_of(j), *scratch[5 * j : 5 * j + 5], e) for j in range(n)]
        waits = []

        def spread(slot, kind, src, dst):
            out_of, into = exchange_views(kind, src, dst, S)
            for k in range(1, S):
                to = lax.rem(me + k, S)
                waits.append(remote(out_of(to), into(me), send.at[slot, k], recv.at[slot, k], shard=to))
                waits[-1].start()
            waits.append(pltpu.make_async_copy(out_of(me), into(me), here.at[slot]))
            waits[-1].start()

        def deliver(j):
            total, kind = sums[j].finish(), chunks[j][1]
            if kind == "keep" or (isinstance(kind, int) and kind == 0):
                waits.append(pltpu.make_async_copy(total, outs[j], here.at[j]))
                waits[-1].start()
            elif isinstance(kind, int):
                to = lax.rem(me + kind, S)
                waits.append(remote(total, outs[j], send.at[j, kind], recv.at[j, kind], shard=to))
                waits[-1].start()
            else:
                spread(j, kind, total, outs[j])

        for i, (kind, _) in enumerate(extra):
            if kind != "plane":
                spread(n + i, kind, more[i], more_outs[i])
                continue
            for k in range(1, E):
                to = lax.rem(e + k, E)
                waits.append(remote(more[i].at[to], more_outs[i].at[e], send.at[n + i, k], recv.at[n + i, k], expert=to))
                waits[-1].start()
            waits.append(pltpu.make_async_copy(more[i].at[e], more_outs[i].at[e], here.at[n + i]))
            waits[-1].start()
        for each in sums:
            each.start()
        for each in sums:
            each.send_diagonal()
        for each in sums:
            each.send_sides()
        for j in range(n):
            deliver(j)
        for copy in waits:
            copy.wait()

    scratch = []
    for a, _ in chunks:
        scratch += PlaneSum.scratch(*a.shape[-2:])
    dma = pltpu.SemaphoreType.DMA
    return pl.pallas_call(
        kernel,
        out_shape=[jax.ShapeDtypeStruct(out_shape(a, kind), a.dtype) for a, kind in chunks]
        + [
            jax.ShapeDtypeStruct(a.shape if kind == "plane" else exchange_shape(kind, a, S), a.dtype)
            for kind, a in extra
        ],
        in_specs=[ANY] * (u + m),
        out_specs=[ANY] * (n + m),
        scratch_shapes=scratch + [dma((n + m, max(S, E))), dma((n + m, max(S, E))), dma((n + m,))],
        compiler_params=pltpu.CompilerParams(
            collective_id=ident, has_side_effects=True, vmem_limit_bytes=48 * 2**20
        ),
    )(*arrays, *[a for _, a in extra])


def hidden_kernel(ident, S, h_side, cot_all, w_exp, w_sh, d_exp, d_sh, shared):
    rows, wide = h_side.shape
    cols = FF_PAD
    T = 2 * rows
    side = wide - D
    hot = 8 * EXP_DEV
    ff = w_exp.shape[1]
    both = EXP_DEV * ff
    rest = cols - both

    def kernel(
        h_ref, c_all, we_hbm, ws_hbm, de_hbm, ds_hbm,
        h_all, out_all, back_sum, in_grad, down_grad, sh_grad, sd_grad,
        wi, wd, acc_in, acc_down, hv, cv, pre, mg, mid, pg, ov, aside,
        mine, stage, core_in, diag_in, side_in, cut,
        send, recv, load, store, fixed, sum_send, sum_recv,
    ):
        me, e = lax.axis_index("shard"), lax.axis_index("expert")
        ec, ex, ey = flip(e, 1), flip(e, 2), flip(e, 4)
        exy = flip(ex, 4)
        greet(
            [{"shard": lax.rem(me + k, S)} for k in range(1, S)]
            + [{"expert": ec}, {"expert": ex}, {"expert": ey}]
        )

        def pull(kind, k, src, at, **where):
            return remote(src, at, send.at[kind, k], recv.at[kind, k], **where)

        def z_copy(k):
            return pull(0, k, h_ref, h_all.at[e, me], shard=lax.rem(me - k + S, S))

        def block(at, k):
            return h_all.at[at, lax.rem(me + k, S)]

        def hop(kind, k):
            if kind in (1, 2, 3):
                at = block(e, k)
                return pull(kind, k, at, at, expert={1: ec, 2: ex, 3: ey}[kind])
            at = block({4: ex, 5: ey, 7: exy}[kind], k)
            return pull(kind, k, at, at, expert=ec)

        def diag(k, by_x):
            at = block(ex if by_x else ey, k)
            return pull(6, k, at, at, expert=ey if by_x else ex)

        own = pltpu.make_async_copy(h_ref, h_all.at[e, me], fixed.at[0])
        def expert_rows(hbm, hbm_down, rows_in, rows_down):
            made = []
            for x in range(EXP_DEV):
                made.append((hbm.at[x, :, pl.ds(0, D)], rows_in.at[pl.ds(x * ff, ff)]))
                made.append((hbm.at[x, :, pl.ds(D, D)], rows_in.at[pl.ds(cols + x * ff, ff)]))
                made.append((hbm_down.at[x], rows_down.at[pl.ds(x * ff, ff)]))
            return made

        loads = expert_rows(we_hbm, de_hbm, wi, wd) + [
            (ws_hbm.at[0], wi.at[pl.ds(both, rest)]),
            (ws_hbm.at[1], wi.at[pl.ds(cols + both, rest)]),
            (ds_hbm, wd.at[pl.ds(both, rest)]),
        ]
        weights = [pltpu.make_async_copy(src, dst, fixed.at[1 + i]) for i, (src, dst) in enumerate(loads)]
        own.start()
        z_copy(1).start()
        for copy in weights:
            copy.start()

        @pl.loop(0, cols // 32)
        def _(i):
            acc_in[pl.ds(pl.multiple_of(i * 64, 64), 64), :] = jnp.zeros((64, D), f32)
            acc_down[pl.ds(pl.multiple_of(i * 32, 32), 32), :] = jnp.zeros((32, D), f32)

        own.wait()

        def out_copies(at, to, k):
            q = lax.rem(me + k, S)
            return [
                pltpu.make_async_copy(ov.at[pl.ds(j * rows, rows)], out_all.at[index, q], store.at[j])
                for j, index in enumerate((at, to))
            ]

        def weight_grads(slot):
            for m in range(2):
                part = pl.ds(m * cols, cols)
                acc_in[part, :] += mm_tn(pg[:, part], hv[slot, :, :D])
            acc_down[...] += mm_tn(mid[...], cv[slot])

        def plane(at, src, dst, **where):
            return remote(src, dst, sum_send.at[at], sum_recv.at[at], **where)

        def to_core(u):
            return plane(u % 2, stage.at[u % 2], core_in.at[u % 2], expert=ec)

        half = rows // 2
        first_half, last_half = pl.ds(0, half), pl.ds(half, half)

        def diagonals(j):
            term = mine.at[j % 2, 3]
            return [
                plane(2, term.at[first_half], diag_in.at[0], expert=ex),
                plane(3, term.at[last_half], diag_in.at[1], expert=ey),
            ]

        def sides(j):
            return [
                plane(4, mine.at[j % 2, 1], side_in.at[0], expert=ex),
                plane(5, mine.at[j % 2, 2], side_in.at[1], expert=ey),
            ]

        def to_owner(j):
            k = chunk(j)
            return plane(6 + k, mine.at[j % 2, 0], back_sum.at[k], shard=lax.rem(me + k, S))

        def add_core(w):
            to_core(w).wait_recv()
            term = mine.at[(w // 4) % 2, w % 4]
            add_into(term, rows, term, core_in.at[w % 2])

        def send_diagonals(j):
            for copy in diagonals(j):
                copy.start()

        def send_sides(j):
            for copy in diagonals(j):
                copy.wait_recv()
            by_x, by_y = mine.at[j % 2, 1, last_half], mine.at[j % 2, 2, first_half]
            add_into(by_x, half, by_x, diag_in.at[1])
            add_into(by_y, half, by_y, diag_in.at[0])
            for copy in sides(j):
                copy.start()

        def finish_sum(j):
            for copy in sides(j):
                copy.wait_recv()
            total = mine.at[j % 2, 0]
            add_into(total, rows, total, side_in.at[0], side_in.at[1])
            for copy in diagonals(j) + sides(j):
                copy.wait_send()

        def unit(at, to, k, u, began):
            q = lax.rem(me + k, S)
            slot = u % 2
            loads = [
                [
                    pltpu.make_async_copy(
                        (h_all, c_all)[a].at[index, q],
                        (hv, cv)[a].at[slot, pl.ds(j * rows, rows)],
                        load.at[a, j],
                    )
                    for j, index in enumerate((at, to))
                ]
                for a in range(2)
            ]
            for pair in loads:
                for copy in pair:
                    copy.start()

            @pl.when(began)
            def _():
                weight_grads(1 - slot)

            for pair in loads:
                for copy in pair:
                    copy.wait()
            pre[...] = mm_nt(hv[slot, :, :D], wi[...])
            mg[...] = mm_nt(cv[slot], wd[...])

            @pl.when(began)
            def _():
                for copy in out_copies(at, to, k):
                    copy.wait()

            step = 64

            @pl.loop(0, T // step)
            def _(i):
                part = pl.ds(pl.multiple_of(i * step, step), step)
                lane = lax.broadcasted_iota(jnp.int32, (step, side), 1)
                w_side = hv[slot, part, D:].astype(f32)

                def weight(x):
                    keep = (lane == EXP_DEV * e + x) | (lane == hot + EXP_DEV * e + x)
                    return jnp.sum(jnp.where(keep, w_side, 0.0), axis=1, keepdims=True)

                w = [weight(x) for x in range(EXP_DEV)]
                lane_c = lax.broadcasted_iota(jnp.int32, (step, 128), 1)
                totals = [jnp.zeros((step, 128), f32) for _ in range(EXP_DEV)]
                for c in range(cols // 128):
                    here_g = slice(c * 128, c * 128 + 128)
                    here_u = slice(cols + c * 128, cols + c * 128 + 128)
                    gate, up, grad = pre[part, here_g], pre[part, here_u], mg[part, here_g]
                    sig = jax.nn.sigmoid(gate)
                    act = gate * sig
                    slope = sig * (1.0 + gate * (1.0 - sig))
                    middle = act * up
                    both_grad = middle * grad
                    factor = None
                    for x in reversed(range(EXP_DEV)):
                        low, high = max(x * ff, c * 128), min((x + 1) * ff, c * 128 + 128)
                        if low >= high:
                            continue
                        if high - low == 128:
                            totals[x] = totals[x] + both_grad
                            factor = w[x]
                        else:
                            inside = (lane_c >= low - c * 128) & (lane_c < high - c * 128)
                            totals[x] = totals[x] + jnp.where(inside, both_grad, 0.0)
                            factor = jnp.where(inside, w[x], 1.0 if factor is None else factor)
                    if factor is not None:
                        grad = grad * factor
                        middle = middle * factor
                    mid[part, here_g] = middle.astype(bf16)
                    pg[part, here_g] = (grad * up * slope).astype(bf16)
                    pg[part, here_u] = (grad * act).astype(bf16)
                sums = [jnp.sum(v, axis=1, keepdims=True) for v in totals]
                high = [v.astype(bf16).astype(f32) for v in sums]
                low = [v - w for v, w in zip(sums, high)]
                made = jnp.zeros((step, side), f32)
                for x in range(2):
                    made = jnp.where(lane == EXP_DEV * e + x, high[x], made)
                    made = jnp.where(lane == hot + EXP_DEV * e + x, low[x], made)
                aside[part, :] = made.astype(bf16)

            ov[...] = mm(mid[...], wd[...]).astype(bf16)
            for copy in out_copies(at, to, k):
                copy.start()

            @pl.when(u >= 2)
            def _():
                to_core(u).wait_send()

            back = mm(pg[...], wi[...]).astype(bf16)
            mine[(u // 4) % 2, u % 4, :, :D] = back[:rows]
            mine[(u // 4) % 2, u % 4, :, D:] = aside[:rows, :]
            stage[slot, :, :D] = back[rows:]
            stage[slot, :, D:] = aside[rows:, :]
            to_core(u).start()

        def chunk(i):
            return (1 + 2 * i) * (1 - i // 2) + 2 * (S - 1 - i) * (i // 2)

        def along(k):
            hop(2, k).start()
            hop(3, k).start()

        def pass_on(v):
            k = chunk(v // 4)

            @pl.when(v % 4 == 0)
            def _():
                hop(1, k).start()

            @pl.when(v % 4 == 1)
            def _():
                @pl.when((v == 1) | (k >= S // 2))
                def _():
                    hop(2, k).wait_recv()

                @pl.when(v == 1)
                def _():
                    diag(k, True).start()

                hop(4, k).start()

            @pl.when(v % 4 == 2)
            def _():
                @pl.when(k < S // 2)
                def _():
                    hop(3, k).wait_recv()

                hop(5, k).start()

            @pl.when(v % 4 == 3)
            def _():
                diag(k, True).wait_recv()
                hop(7, k).start()

        def to_diagonal(k):
            @pl.when(k < S // 2)
            def _():
                hop(2, k).wait_recv()
                diag(k, True).start()

            @pl.when(k >= S // 2)
            def _():
                hop(3, k).wait_recv()
                diag(k, False).start()

        z_copy(1).wait_send()
        z_copy(3).start()
        z_copy(1).wait_recv()
        along(1)
        hop(1, 1).start()
        for copy in weights:
            copy.wait()

        units = 4 * S

        @pl.loop(0, units)
        def _(u):
            i, g = u // 4, u % 4
            k = chunk(i)

            @pl.when(u > 0)
            def _():
                add_core(u - 1)

            @pl.when((i > 1) & (g == 0))
            def _():
                to_owner(i - 2).wait_send()

            @pl.when(i > 0)
            def _():
                j = i - 1

                @pl.when(g == 0)
                def _():
                    send_diagonals(j)

                @pl.when(g == 1)
                def _():
                    send_sides(j)

                @pl.when(g == 3)
                def _():
                    finish_sum(j)
                    to_owner(j).start()

            @pl.when((u > 0) & (u < units - 1))
            def _():
                pass_on(u + 1)

            @pl.when((g == 3) & (i < S - 1))
            def _():
                to_diagonal(chunk(i + 1))

            @pl.when((g == 1) & (i < S - 1))
            def _():
                later = chunk(i + 1)

                @pl.when(later > 0)
                def _():
                    z_copy(later).wait_send()

                    @pl.when(i == 0)
                    def _():
                        z_copy(2).start()

                    z_copy(later).wait_recv()

                along(later)

            for kind, at in ((1, 0), (4, 1), (5, 2), (7, 3)):
                @pl.when(g == at)
                def _(kind=kind):
                    hop(kind, k).wait_recv()

            at = e + (g % 2) * (ex - e) + (g // 2) * (ey - e)
            unit(at, flip(at, 1), k, u, u > 0)

            @pl.when(u == 0)
            def _():
                pass_on(1)

        last_sum = S - 1
        add_core(units - 1)
        send_diagonals(last_sum)
        weight_grads(1)
        results = [(dst, src) for src, dst in expert_rows(in_grad, down_grad, acc_in, acc_down)] + [
            (acc_down.at[pl.ds(both, shared)], sd_grad),
        ]
        last = [pltpu.make_async_copy(src, dst, fixed.at[1 + i]) for i, (src, dst) in enumerate(results)]
        for copy in last:
            copy.start()
        send_sides(last_sum)
        lane = lax.broadcasted_iota(jnp.int32, (shared, 128), 1)
        for n in range(D // 128):
            lanes = slice(n * 128, n * 128 + 128)
            gate, up = acc_in[both : both + shared, lanes], acc_in[cols + both : cols + both + shared, lanes]
            even = jnp.where(lane < 64, gate, pltpu.roll(up, 64, 1))
            odd = jnp.where(lane < 64, pltpu.roll(gate, 64, 1), up)
            for b, v in ((2 * n, even), (2 * n + 1, odd)):
                cut[b % S, b // S] = v.astype(bf16)
        handed = []
        for k in range(1, S):
            to = lax.rem(me + k, S)
            handed.append(
                remote(cut.at[to], sh_grad.at[me], sum_send.at[6 + S + k], sum_recv.at[6 + S + k], shard=to)
            )
        handed.append(pltpu.make_async_copy(cut.at[me], sh_grad.at[me], fixed.at[9]))
        for copy in handed:
            copy.start()
        last += handed
        for k in range(S):
            for kind in (1, 2, 3, 4, 5, 7):
                hop(kind, k).wait_send()
            diag(k, k < S // 2).wait_send()
        to_owner(last_sum - 1).wait_send()
        for w in (units - 2, units - 1):
            to_core(w).wait_send()
        for copy in out_copies(exy, flip(exy, 1), 0):
            copy.wait()
        finish_sum(last_sum)
        kept = pltpu.make_async_copy(mine.at[last_sum % 2, 0], back_sum.at[0], fixed.at[0])
        kept.start()
        for j in range(S - 1):
            to_owner(j).wait_recv()
        kept.wait()
        for copy in last:
            copy.wait()

    dma = pltpu.SemaphoreType.DMA
    shape = jax.ShapeDtypeStruct
    macs = 8 * S * rows * D * cols * 9
    return pl.pallas_call(
        kernel,
        out_shape=[
            shape((8, S, rows, wide), bf16),
            shape((8, S, rows, D), bf16),
            shape((S, rows, wide), bf16),
            shape(w_exp.shape, f32),
            shape(d_exp.shape, f32),
            shape((S, 8, shared, 128), bf16),
            shape((shared, D), f32),
        ],
        in_specs=[ANY] * 6,
        out_specs=[ANY] * 7,
        scratch_shapes=[
            pltpu.VMEM((2 * cols, D), bf16),
            pltpu.VMEM((cols, D), bf16),
            pltpu.VMEM((2 * cols, D), f32),
            pltpu.VMEM((cols, D), f32),
            pltpu.VMEM((2, T, wide), bf16),
            pltpu.VMEM((2, T, D), bf16),
            pltpu.VMEM((T, 2 * cols), f32),
            pltpu.VMEM((T, cols), f32),
            pltpu.VMEM((T, cols), bf16),
            pltpu.VMEM((T, 2 * cols), bf16),
            pltpu.VMEM((T, D), bf16),
            pltpu.VMEM((T, side), bf16),
            pltpu.VMEM((2, 4, rows, wide), bf16),
            pltpu.VMEM((2, rows, wide), bf16),
            pltpu.VMEM((2, rows, wide), bf16),
            pltpu.VMEM((2, rows // 2, wide), bf16),
            pltpu.VMEM((2, rows, wide), bf16),
            pltpu.VMEM((S, 8, shared, 128), bf16),
            dma((8, S)),
            dma((8, S)),
            dma((2, 2)),
            dma((2,)),
            dma((10,)),
            dma((6 + 2 * S,)),
            dma((6 + 2 * S,)),
        ],
        compiler_params=pltpu.CompilerParams(
            collective_id=ident, has_side_effects=True, vmem_limit_bytes=60 * 2**20
        ),
        cost_estimate=pl.CostEstimate(flops=2 * macs, bytes_accessed=10**8, transcendentals=10**6),
    )(h_side, cot_all, w_exp, w_sh, d_exp, d_sh)[1:]


def local(
    block_in,
    cotangent,
    doc_ids,
    routes,
    attn_gain,
    query_weight,
    kv_down_weight,
    kv_gain,
    kv_up_weight,
    out_weight,
    ffn_gain,
    router_weight,
    shared_in,
    shared_down,
    expert_in,
    expert_down,
):
    tok = block_in.shape[0]
    E, S = lax.axis_size("expert"), lax.axis_size("shard")
    e, s = lax.axis_index("expert"), lax.axis_index("shard")
    group = tok * S
    heads = HEADS // S
    units = SH_FF // (E * S)
    experts_all = EXP_DEV * E
    ff = expert_in.shape[2]
    first = s * tok
    scale = QK ** (-0.5)

    experts_cols = jnp.arange(experts_all, dtype=jnp.int32)

    def own(v):
        return lax.dynamic_slice_in_dim(v, first, tok, 0)

    def at_row(v, row):
        return jnp.pad(v, ((row, 16 + experts_all - row - v.shape[0]), (0, D // S - v.shape[1])))

    small = at_row(attn_gain[None], 0) + at_row(ffn_gain[None], 1) + at_row(kv_gain[None], 2)
    small = small + at_row(router_weight.T, 16)
    w_exp, d_exp = expert_in.transpose(0, 2, 1), expert_down.transpose(0, 2, 1)
    if KV_RANK // S // E >= 16:
        cot_all = lax.all_gather(cotangent, BOTH, axis=0, tiled=True)
        weights = [(query_weight, True), (kv_down_weight, False), (kv_up_weight, True)]
        x_rows, small, w_q, kv_down, kv_up = fetch_weights(0, E, S, block_in, small, weights)
    else:
        x_rows, small, w_q, kv_down, kv_up = shard_exchange(
            0,
            S,
            ("rows", block_in),
            ("rows", small),
            ("cols_to_rows", query_weight),
            ("rows", kv_down_weight),
            ("cols_to_rows", kv_up_weight),
        )
    small = small.reshape(S, 16 + experts_all, D // S)
    gain_a, gain_f = small[:, 0].reshape(D), small[:, 1].reshape(D)
    gain_k = small[:, 2, : KV_RANK // S].reshape(KV_RANK)
    router = small[:, 16:].transpose(1, 0, 2).reshape(experts_all, D)

    shared_in, shared_down, x_rows = lax.optimization_barrier((shared_in, shared_down, x_rows))
    rest = FF_PAD - EXP_DEV * ff
    if E == 8:
        sends = shared_rows(shared_in, S * units)
    else:
        sends = jnp.stack(
            [lax.dynamic_slice_in_dim(shared_in, at + e * S * units, S * units, 1).T for at in (0, SH_FF)]
        )
    sends = sends.reshape(2, S, units, D // S)
    w_sh = jnp.zeros((2, rest, D), bf16)
    for k in range(S):
        part = lax.dynamic_index_in_dim(sends, (s - k) % S, 1, keepdims=False)
        if k:
            part = lax.ppermute(part, "shard", [(i, (i - k) % S) for i in range(S)])
        w_sh = lax.dynamic_update_slice(w_sh, part, (0, 0, (s + k) % S * (D // S)))
    rows_here = shared_down.shape[0]
    holder = [i * S * units // rows_here for i in range(E)]

    def send_rows(to):
        at = jnp.clip((e * S + to) * units - s * rows_here, 0, rows_here - units)
        return lax.dynamic_slice_in_dim(shared_down, at, units, 0)

    mine = (e * S * units // rows_here) == s
    sh_down = jnp.where(mine, send_rows(s), 0)
    for k in range(1, S):
        pairs = [(i * S + holder[i], i * S + (holder[i] + k) % S) for i in range(E)]
        sh_down = sh_down + lax.ppermute(send_rows((s + k) % S), BOTH, pairs)

    d_sh = jnp.pad(sh_down, ((0, rest - units), (0, 0)))

    doc_row = doc_ids[0]
    cosine, sine = rope_tables(doc_row)
    index = jnp.arange(group, dtype=jnp.int32)
    allowed = (doc_row[:, None] == doc_row[None, :]) & (index[None, :] <= index[:, None])
    x_float = x_rows.astype(f32)
    scale_in = inv_rms(x_float)
    x_norm = (x_float * scale_in * gain_a).astype(bf16)
    query_raw = lax.optimization_barrier(mm(x_norm, w_q)).reshape(group, heads, QK)
    queries = jnp.concatenate(
        [
            query_raw[..., :NOPE],
            rotate(query_raw[..., NOPE:], cosine[:, None, :], sine[:, None, :]),
        ],
        axis=-1,
    ).astype(bf16)
    latent_raw = mm(x_norm, kv_down)
    compressed = latent_raw[:, :KV_RANK]
    scale_kv = inv_rms(compressed)
    latent = (compressed * scale_kv * gain_k).astype(bf16)
    key_rope = rotate(latent_raw[:, KV_RANK:], cosine, sine).astype(bf16)
    expanded = mm(latent, kv_up).astype(bf16).reshape(group, heads, NOPE + VDIM)
    keys = jnp.concatenate(
        [expanded[..., :NOPE], jnp.broadcast_to(key_rope[:, None, :], (group, heads, ROPE))], axis=-1
    )
    values = expanded[..., NOPE:]
    scores = jnp.einsum("qhd,khd->hqk", queries, keys, preferred_element_type=f32)
    scores = jnp.where(allowed[None], scores * scale, -jnp.inf)
    row_max = jnp.max(scores, axis=-1, keepdims=True)
    lse = row_max + jnp.log(jnp.sum(jnp.exp(scores - row_max), axis=-1, keepdims=True))
    probs = jnp.exp(scores - lse)
    probs_low = probs.astype(bf16)
    attended = (
        jnp.einsum("hqk,khd->qhd", probs_low, values, preferred_element_type=f32)
        .astype(bf16)
        .reshape(group, heads * VDIM)
    )
    attended, w_sh, d_sh = lax.optimization_barrier((attended, w_sh, d_sh))
    (resid_terms,) = shard_exchange(1, S, ("blocks", mm(attended, out_weight).astype(bf16)))

    resid = block_in.astype(f32) + jnp.sum(resid_terms.reshape(S, tok, D).astype(f32), axis=0)
    scale_ffn = inv_rms(resid)
    h_norm = (resid * scale_ffn * gain_f).astype(bf16)
    logits = mm_nt(h_norm, router)
    named = jnp.any(routes[:, :, None] == experts_cols[None, None, :], axis=1)
    masked = jnp.where(named, logits, -jnp.inf)
    top = jnp.exp(masked - jnp.max(masked, axis=-1, keepdims=True))
    route_w = top / jnp.sum(top, axis=-1, keepdims=True)
    w_high = route_w.astype(bf16)
    w_low = (route_w - w_high.astype(f32)).astype(bf16)
    side = -(-2 * experts_all // 128) * 128
    h_side = jnp.concatenate([h_norm, w_high, w_low, jnp.zeros((tok, side - 2 * experts_all), bf16)], axis=1)

    unit_at = slice(EXP_DEV * ff, EXP_DEV * ff + units)
    spot = (
        (e * EXP_DEV + jnp.arange(EXP_DEV, dtype=jnp.int32))[:, None] == experts_cols[None, :]
    ).astype(f32)

    def hidden_units(h_all, cot_all):
        count = h_all.shape[0]
        w_in = jnp.concatenate(
            [v for j in range(2) for v in (*w_exp[:, :, j * D : (j + 1) * D], w_sh[j])], axis=0
        )
        w_down = jnp.concatenate([*d_exp, d_sh], axis=0)
        w_all = h_all[:, D : D + experts_all].astype(f32) + h_all[:, D + experts_all : D + 2 * experts_all].astype(f32)
        w_cols = lax.dot_general(w_all, spot, (((1,), (1,)), ((), ())), precision=lax.Precision.HIGHEST)
        h_all = h_all[:, :D]
        weight = jnp.concatenate(
            [
                jnp.broadcast_to(w_cols[:, :1], (count, ff)),
                jnp.broadcast_to(w_cols[:, 1:], (count, ff)),
                jnp.ones((count, rest), f32),
            ],
            axis=1,
        )
        pre = mm_nt(h_all, w_in)
        gate_pre, up_pre = pre[:, :FF_PAD], pre[:, FF_PAD:]
        mid_grad = mm_nt(cot_all, w_down)
        sigmoid = jax.nn.sigmoid(gate_pre)
        act = gate_pre * sigmoid
        slope = sigmoid * (1.0 + gate_pre * (1.0 - sigmoid))
        mid = act * up_pre
        mid_low = (weight * mid).astype(bf16)
        weighted = weight * mid_grad
        gate_grad = (weighted * up_pre * slope).astype(bf16)
        up_grad = (weighted * act).astype(bf16)
        product = mid * mid_grad
        wg = jnp.stack([jnp.sum(product[:, k * ff : (k + 1) * ff], axis=1) for k in range(EXP_DEV)], axis=1)
        out_part = mm(mid_low, w_down).astype(bf16)
        pre_grad = jnp.concatenate([gate_grad, up_grad], axis=1)
        back_part = mm(pre_grad, w_in).astype(bf16)
        in_grad = jnp.stack(
            [
                jnp.concatenate([mm_tn(h_all, g[:, k * ff : (k + 1) * ff]) for g in (gate_grad, up_grad)], axis=0)
                for k in range(EXP_DEV)
            ]
        )
        down_grad = jnp.stack([mm_tn(cot_all, mid_low[:, k * ff : (k + 1) * ff]) for k in range(EXP_DEV)])
        sh_down_grad = mm_tn(mid_low[:, unit_at], cot_all)
        sh_in_grad = jnp.stack([mm_tn(g[:, unit_at], h_all) for g in (gate_grad, up_grad)])
        wg_all = lax.dot_general(wg, spot, (((1,), (0,)), ((), ())), precision=lax.Precision.HIGHEST)
        wg_high = wg_all.astype(bf16)
        wg_low = (wg_all - wg_high.astype(f32)).astype(bf16)
        back_part = jnp.concatenate(
            [back_part, wg_high, wg_low, jnp.zeros((count, side - 2 * experts_all), bf16)], axis=1
        )
        return ((in_grad, down_grad, sh_down_grad, sh_in_grad), (back_part, out_part))

    if E == 8:
        made = hidden_kernel(2, S, h_side, cot_all.reshape(E, S, tok, D), w_exp, w_sh, d_exp, d_sh, units)
        out_all, back_terms, expert_in_grad, expert_down_grad, sh_rows, shared_down_grad = made
        expert_in_grad, expert_down_grad = expert_in_grad.transpose(0, 2, 1), expert_down_grad.transpose(0, 2, 1)
        back_sum = jnp.sum(back_terms.astype(f32), axis=0)
    else:
        pieces = E // 8
        rows_in = [v.reshape(pieces, -1, v.shape[-1]) for v in (h_side, cotangent)]

        def one(total, rows):
            made, parts = hidden_units(*[lax.all_gather(v, BOTH, axis=0, tiled=True) for v in rows])
            sums = [lax.psum_scatter(v.astype(bf16), BOTH, scatter_dimension=0, tiled=True).astype(f32) for v in parts]
            return (jax.tree.map(jnp.add, total, made), sums)

        zeros = (
            jnp.zeros(expert_in.shape, f32),
            jnp.zeros(expert_down.shape, f32),
            jnp.zeros((units, D), f32),
            jnp.zeros((2, units, D), f32),
        )
        grads, sums = lax.scan(one, zeros, tuple(rows_in))
        back_sum, routed = [v.reshape(-1, v.shape[-1]) for v in sums]
        expert_in_grad, expert_down_grad, shared_down_grad, sh_in_grad = grads
    hidden_grad = back_sum[:, :D]
    weight_grad = back_sum[:, D : D + experts_all] + back_sum[:, D + experts_all : D + 2 * experts_all]

    logit_grad = (route_w * (weight_grad - jnp.sum(route_w * weight_grad, axis=-1, keepdims=True))).astype(bf16)
    router_grad = mm_tn(h_norm, logit_grad)
    hidden_grad = hidden_grad + mm(logit_grad, router)
    resid_part, ffn_gain_grad = norm_back(hidden_grad, resid, scale_ffn, gain_f)
    resid_grad = cotangent.astype(f32) + resid_part
    resid_low = resid_grad.astype(bf16)

    moves = [("rows", resid_low)]
    if E == 8:
        out_one, out_two, resid_rows = reduce_weights(4, E, S, [(out_all, 1), (out_all, 0)], moves)
        sh_rows, resid_rows = lax.optimization_barrier((sh_rows, resid_rows))
        sh_rows = sh_rows.transpose(1, 0, 2, 3)
    else:
        (resid_rows,) = shard_exchange(4, S, *moves)
        sh_sends = sh_in_grad.astype(bf16).reshape(2 * units, E * S, D // (E * S)).transpose(1, 0, 2)
        sh_rows = lax.all_to_all(sh_sends, BOTH, split_axis=0, concat_axis=0, tiled=True)
        shared_in_grad = (
            sh_rows.reshape(E * S, 2, units, D // (E * S))
            .transpose(3, 1, 0, 2)
            .reshape(D // (E * S), 2 * SH_FF)
            .astype(f32)
        )
    att_grad = mm_nt(resid_rows, out_weight).astype(bf16).reshape(group, heads, VDIM)
    out_grad = mm_tn(attended, resid_rows)

    values_grad = jnp.einsum("hqk,qhd->khd", probs_low, att_grad, preferred_element_type=f32)
    probs_grad = jnp.einsum("qhd,khd->hqk", att_grad, values, preferred_element_type=f32)
    delta = jnp.sum(probs * probs_grad, axis=-1, keepdims=True)
    score_grad = lax.optimization_barrier((probs * (probs_grad - delta) * scale).astype(bf16))
    q_grad = jnp.einsum("hqk,khd->qhd", score_grad, keys, preferred_element_type=f32)
    k_grad = jnp.einsum("hqk,qhd->khd", score_grad, queries, preferred_element_type=f32)
    rope_part = jnp.sum(k_grad[..., NOPE:], axis=1)
    key_grad = (
        jnp.concatenate([k_grad[..., :NOPE], values_grad], axis=-1)
        .reshape(group, heads * (NOPE + VDIM))
        .astype(bf16)
    )
    query_grad = (
        jnp.concatenate(
            [q_grad[..., :NOPE], unrotate(q_grad[..., NOPE:], cosine[:, None, :], sine[:, None, :])], axis=-1
        )
        .reshape(group, heads * QK)
        .astype(bf16)
    )
    latent_part = jnp.concatenate([mm_nt(key_grad, kv_up), rope_part, jnp.zeros((group, ROPE), f32)], axis=1)
    norm_part = mm_nt(query_grad, w_q)
    (latent_back,) = shard_exchange(5, S, ("blocks", latent_part.astype(bf16)))
    norm_low = norm_part.astype(bf16)
    latent_back = jnp.sum(latent_back.reshape(S, tok, -1).astype(f32), axis=0)
    compressed_grad, kv_gain_grad = norm_back(latent_back[:, :KV_RANK], own(compressed), own(scale_kv), gain_k)
    latent_grad = jnp.concatenate(
        [compressed_grad, unrotate(latent_back[:, KV_RANK : KV_RANK + ROPE], own(cosine), own(sine))], axis=1
    ).astype(bf16)
    norm_own = mm_nt(latent_grad, kv_down)
    x_own, scale_x = block_in.astype(f32), own(scale_in)
    attn_gain_grad = jnp.sum(norm_part * x_float * scale_in, axis=0) + jnp.sum(norm_own * x_own * scale_x, axis=0)

    rows, kv_rows = D // (E * S), KV_RANK // (E * S)
    q_w_grad = mm_tn(x_norm, query_grad)
    kv_up_grad = mm_tn(latent, key_grad)
    (latent_grad_rows,) = shard_exchange(6, S, ("rows", latent_grad))
    x_cols = lax.dynamic_slice_in_dim(x_norm, s * (D // S), D // S, 1)
    kv_down_grad = mm_tn(x_cols, latent_grad_rows)
    def lanes(v, *more):
        v = v.reshape((E, S, 1, -1)) if v.ndim == 1 else v
        if more:
            v = jnp.concatenate([v, more[0].reshape(E, S, 1, -1)], axis=-1)
        return jnp.pad(v, ((0, 0), (0, 0), (0, 0), (0, 128 - v.shape[-1])))

    gains = jnp.concatenate(
        [
            lanes(attn_gain_grad, kv_gain_grad),
            lanes(ffn_gain_grad),
            lanes(router_grad.reshape(E, S, rows, experts_all).transpose(0, 1, 3, 2)),
        ],
        axis=2,
    ).astype(bf16)
    gain_count = -(-gains.shape[2] // 8) * 8
    gains = jnp.pad(gains, ((0, 0), (0, 0), (0, gain_count - gains.shape[2]), (0, 0))).reshape(E, S * gain_count, 128)

    def cut(g):
        return g.astype(bf16).reshape(E, g.shape[0] // E, g.shape[1])

    q_parts, up_parts, out_parts, down_parts = cut(q_w_grad), cut(kv_up_grad), cut(out_grad), cut(kv_down_grad)
    if E == 8:
        (
            out_three,
            out_four,
            query_weight_grad,
            mine_out,
            kv_up_weight_grad,
            mine_down,
            gain_sums,
            norm_terms,
            sh_rows,
        ) = reduce_weights(
            7,
            E,
            S,
            [
                (out_all, 2),
                (out_all, 3),
                (q_parts, "rows_to_cols"),
                (out_parts, "keep"),
                (up_parts, "rows_to_cols"),
                (down_parts, "keep"),
                (gains, "rows"),
            ],
            [("blocks", norm_low), ("plane", sh_rows)],
        )
        sh_rows = sh_rows.reshape(E * S * units, -1).T
        shared_in_grad = jnp.concatenate([sh_rows[: D // (E * S)], sh_rows[D // (E * S) :]], axis=1).astype(f32)
        routed = sum(v.astype(f32) for v in (out_one, out_two, out_three, out_four))
    else:
        sums = [
            lax.psum_scatter(v, "expert", scatter_dimension=0, tiled=False)
            for v in (gains, down_parts, out_parts, q_parts, up_parts)
        ]
        gain_sums, mine_down, mine_out = lax.all_gather(sums[0], "shard", axis=0, tiled=True), sums[1], sums[2]
        query_weight_grad, kv_up_weight_grad = [
            lax.all_to_all(v, "shard", split_axis=0, concat_axis=1, tiled=True) for v in sums[3:]
        ]
        (norm_terms,) = shard_exchange(7, S, ("blocks", norm_low))
    pairs = [(ee * S + ss, E * ss + ee) for ee in range(E) for ss in range(S)]
    out_weight_grad = lax.ppermute(mine_out, BOTH, pairs).astype(f32)
    kv_down_weight_grad = lax.ppermute(mine_down, BOTH, pairs).astype(f32)
    block_out = resid + routed
    gain_sums = gain_sums.reshape(S, S, gain_count, 128)
    gain_sums = lax.dynamic_index_in_dim(gain_sums, s, 1, keepdims=False)
    gain_sums = jnp.sum(gain_sums.astype(f32), axis=0)
    norm_grad = norm_own + jnp.sum(norm_terms.reshape(S, tok, D).astype(f32), axis=0)
    scaled = norm_grad * gain_a
    input_grad = resid_grad + (
        scale_x * scaled - x_own * scale_x**3 * jnp.mean(scaled * x_own, axis=-1, keepdims=True)
    )

    return (
        block_out,
        input_grad,
        gain_sums[0, :rows],
        query_weight_grad.astype(f32),
        kv_down_weight_grad,
        gain_sums[0, rows : rows + kv_rows],
        kv_up_weight_grad.astype(f32),
        out_weight_grad,
        gain_sums[1, :rows],
        gain_sums[2 : 2 + experts_all, :rows].T,
        shared_in_grad,
        shared_down_grad,
        expert_in_grad,
        expert_down_grad,
    )


def solution(mesh):
    tokens = P(BOTH, None)
    shard = P("shard", None)
    in_specs = (
        tokens,
        tokens,
        P("expert", None),
        tokens,
        P("shard"),
        shard,
        shard,
        P("shard"),
        shard,
        shard,
        P("shard"),
        shard,
        shard,
        shard,
        P("expert", None, "shard"),
        P("expert", None, "shard"),
    )
    out_specs = (
        tokens,
        tokens,
        P(BOTH),
        tokens,
        tokens,
        P(BOTH),
        tokens,
        tokens,
        P(BOTH),
        tokens,
        tokens,
        tokens,
        P("expert", None, "shard"),
        P("expert", None, "shard"),
    )
    return jax.shard_map(local, mesh=mesh, in_specs=in_specs, out_specs=out_specs, check_vma=False)
```
